32 devices in a mesh: groups: 2 (over x), gx: 16 (over z, y, core).
Axes of the slice: x: 2, y: 2, z: 4, core: 2. Of those that a mesh axis runs over, the one named last changes fastest.
Arguments:
- snapshots: bfloat16 [256, 4, 512, 128], P('gx', None, 'groups'), parts along dimension 2, may hold values from -20 to 20
- cell_weights: float32 [512, 128], P(('groups', 'gx')), parts along dimension 0, may hold values from 0.5 to 4.5
- diffusivity: float32 [4, 512, 128], P(None, ('groups', 'gx')), parts along dimension 1, may hold values from 0.2 to 2
Outputs:
- diffused_modes: bfloat16 [256, 4, 512, 128], P(None, None, ('groups', 'gx')), parts along dimension 2
- reduced_operator: float32 [512, 256], P('groups'), parts along dimension 0
The draws below stay inside these ranges and needn't reach their ends.
There are 2 independent parts, one for each index of `groups`. The reference program is written for one: setup_inputs(seed, part) draws one part's arguments, and reference() takes and returns one part's arrays. A program takes and returns all parts, laid end to end along the dimension named above; each array names one. Nothing has to cross between parts.
All inputs are finite; a program needn't handle non-finite values.
Results may differ from the reference program's by a relative error of at most 0.0005.
Values may be sent and summed in bfloat16 or wider, within the bound.
No kernel may reach another device: no remote copies, remote signals or barrier semaphores. Data moves between devices by JAX's collectives and lax.ppermute only.
A program may use at most 128 MiB of HBM per device.

```python
import math
import jax
import jax.numpy as jnp
from jax import lax

S = 256
V = 4
PY = 128
NX = 256


def draw_snapshots(key, part):
    keys = jax.random.split(key, 4)
    amplitude = jnp.exp(jax.random.uniform(keys[0], (S, 1, 1, 1), minval=0.0, maxval=math.log(3.0)))
    noise = jax.random.truncated_normal(keys[1], -4.0, 4.0, (S, V, NX, PY))
    coeffs = jax.random.uniform(keys[2], (4, S, 1, 1, 1), minval=-0.6, maxval=0.6)
    pattern = jax.random.uniform(keys[3], (4, 1, V, NX, PY), minval=-1.0, maxval=1.0)
    shared = coeffs[0] * pattern[0] + coeffs[1] * pattern[1] + coeffs[2] * pattern[2] + coeffs[3] * pattern[3]
    return (amplitude * (noise + shared)).astype(jnp.bfloat16)


def draw_cell_weights(key, part):
    ramp = 1.0 + 2.0 * jnp.arange(NX, dtype=jnp.float32)[:, None] / (NX - 1)
    factor = jax.random.uniform(key, (NX, PY), minval=0.5, maxval=1.5)
    return ramp * factor


def shard_levels(rng, extent, shards, smallest, largest):
    def one(axis_at, parts):
        heights = jax.random.uniform(jax.random.fold_in(jax.random.fold_in(rng, 6), axis_at), (parts,), jnp.float32, smallest / len(shards), largest / len(shards))
        return jnp.repeat(jnp.exp(heights), extent[axis_at] // parts).reshape((-1,) + (1,) * (len(extent) - axis_at - 1))

    level = one(*shards[0])
    for cut in shards[1:]:
        level = level * one(*cut)
    return level


def setup_inputs(seed: int = 0, part: int = 0) -> dict:
    arg_keys = jax.random.split(jax.random.key(seed), 4)
    own_keys = jax.random.split(jax.random.fold_in(arg_keys[3], part), 4)
    snapshots = draw_snapshots(jax.random.fold_in(jax.random.fold_in(arg_keys[3], part), 71), part)
    cell_weights = draw_cell_weights(jax.random.fold_in(jax.random.fold_in(arg_keys[3], part), 71), part)
    diffusivity = jnp.clip(jnp.exp(math.log(2.0) - 2.3025851 * jax.random.uniform(own_keys[2], (V, NX, PY), jnp.float32) ** shard_levels(own_keys[2], (V, NX, PY), ((1, 16),), -0.2, 0.2)), 0.2, 2.0)
    return {"snapshots": snapshots, "cell_weights": cell_weights, "diffusivity": diffusivity}


def stencil_apply(padded_x, diffusivity):
    field = padded_x[:, :, 2:-2]
    along_x = (-padded_x[:, :, :-4] + 16.0 * padded_x[:, :, 1:-3] - 30.0 * field + 16.0 * padded_x[:, :, 3:-1] - padded_x[:, :, 4:]) / 12.0
    padded_y = jnp.pad(field, ((0, 0), (0, 0), (0, 0), (2, 2)))
    along_y = (-padded_y[..., :-4] + 16.0 * padded_y[..., 1:-3] - 30.0 * field + 16.0 * padded_y[..., 3:-1] - padded_y[..., 4:]) / 12.0
    return diffusivity * (along_x + along_y)

def reference(snapshots, cell_weights, diffusivity):
    hi = lax.Precision.HIGHEST
    cell_count = snapshots.shape[1] * snapshots.shape[2] * snapshots.shape[3]
    snap_float = snapshots.astype(jnp.float32)
    gram_total = jnp.einsum('svxy,tvxy->st', snap_float, snap_float * cell_weights, precision=hi) / cell_count
    lower_factor = jnp.linalg.cholesky(gram_total)
    identity = jnp.eye(gram_total.shape[0], dtype=jnp.float32)
    rotation = jax.scipy.linalg.solve_triangular(lower_factor, identity, lower=True)
    mode_field = jnp.einsum('st,tvxy->svxy', rotation, snap_float, precision=hi)
    padded_x = jnp.pad(mode_field, ((0, 0), (0, 0), (2, 2), (0, 0)))
    diffused = stencil_apply(padded_x, diffusivity)
    reduced = jnp.einsum('svxy,tvxy->st', mode_field * cell_weights, diffused, precision=hi) / cell_count
    return (diffused.astype(jnp.bfloat16), reduced)
```

```python
import jax
import jax.numpy as jnp
from jax import lax
from jax.experimental import pallas as pl
from jax.experimental.pallas import tpu as pltpu
from jax.sharding import PartitionSpec as P

VMEM_LIMIT = 48 * 1024 * 1024
NT = (((1,), (1,)), ((), ()))


def params():
    return pltpu.CompilerParams(vmem_limit_bytes=VMEM_LIMIT)


def split(value):
    high = value.astype(jnp.bfloat16)
    low = (value - high.astype(jnp.float32)).astype(jnp.bfloat16)
    return high, low


def matmul(a, b):
    return jnp.dot(a, b, preferred_element_type=jnp.float32)


def matmul_nt(a, b):
    return lax.dot_general(a, b, NT, preferred_element_type=jnp.float32)


def relayout_kernel(in_ref, out_ref):
    variables = in_ref.shape[1]
    for v in range(variables):
        block = in_ref[:, v].astype(jnp.float32)
        out_ref[0, :, v] = jnp.swapaxes(block, 0, 1).astype(out_ref.dtype)


def relayout(snapshots, owners):
    count, variables, cells, width = snapshots.shape
    rows = cells // owners
    if count % 16 or rows % 16:
        block = snapshots.reshape(count, variables, owners, rows, width)
        return block.transpose(2, 3, 1, 0, 4)
    return pl.pallas_call(
        relayout_kernel,
        grid=(owners,),
        in_specs=[pl.BlockSpec((count, variables, rows, width), lambda i: (0, 0, i, 0))],
        out_specs=pl.BlockSpec((1, rows, variables, count, width), lambda i: (i, 0, 0, 0, 0)),
        out_shape=jax.ShapeDtypeStruct((owners, rows, variables, count, width), snapshots.dtype),
        compiler_params=params(),
        name="relayout",
    )(snapshots)


def row_of(ref, x):
    value = ref[:, x, 0]
    return value.reshape(value.shape[0] * value.shape[1], value.shape[2])


def gram_kernel(x_ref, w_ref, out_ref):
    rows = x_ref.shape[1]

    @pl.when(pl.program_id(0) == 0)
    def _():
        out_ref[...] = jnp.zeros_like(out_ref)

    total = None
    for first in range(0, rows, 4):
        group = range(first, first + 4)
        plain = jnp.concatenate([row_of(x_ref, x) for x in group], axis=1)
        weight = jnp.concatenate([w_ref[x : x + 1, :] for x in group], axis=1)
        high, low = split(plain.astype(jnp.float32) * weight)
        term = matmul_nt(high, plain) + matmul_nt(low, plain)
        total = term if total is None else total + term
    out_ref[...] += total


def gram_of(block, weights):
    owners, rows, variables, count, width = block.shape
    size = owners * count
    return pl.pallas_call(
        gram_kernel,
        grid=(variables,),
        in_specs=[
            pl.BlockSpec((owners, rows, 1, count, width), lambda v: (0, 0, v, 0, 0)),
            pl.BlockSpec((rows, width), lambda v: (0, 0)),
        ],
        out_specs=pl.BlockSpec((size, size), lambda v: (0, 0)),
        out_shape=jax.ShapeDtypeStruct((size, size), jnp.float32),
        compiler_params=params(),
        cost_estimate=pl.CostEstimate(
            flops=4 * size * size * rows * variables * width,
            bytes_accessed=2 * size * rows * variables * width,
            transcendentals=0,
        ),
        name="gram",
    )(block, weights)


def cross_kernel(x_ref, low_ref, high_ref, w_ref, d_ref, band_ref, cross_ref, f_ref):
    rows = x_ref.shape[1]

    @pl.when(pl.program_id(0) == 0)
    def _():
        cross_ref[...] = jnp.zeros_like(cross_ref)

    def row(x):
        if x < 0:
            return row_of(low_ref, x + 2)
        if x >= rows:
            return row_of(high_ref, x - rows)
        return row_of(x_ref, x)

    total = None
    for x in range(0, rows, 2):
        near = jnp.concatenate([row(x + k) for k in range(-2, 4)], axis=1)
        plain = jnp.concatenate([row(x), row(x + 1)], axis=1)
        scale = jnp.concatenate([d_ref[0, x : x + 1, :], d_ref[0, x + 1 : x + 2, :]], axis=1)
        weight = jnp.concatenate([w_ref[x : x + 1, :], w_ref[x + 1 : x + 2, :]], axis=1)
        field = matmul(near, band_ref[...]) * (scale * (1.0 / 12.0))
        high, low = split(field)
        f_ref[0, 0, x // 2] = high
        f_ref[1, 0, x // 2] = low
        high, low = split(field * weight)
        term = matmul_nt(plain, high) + matmul_nt(plain, low)
        total = term if total is None else total + term
    cross_ref[...] += total


def band_matrix(width):
    i = lax.broadcasted_iota(jnp.int32, (6, width, 2, width), 0)
    y = lax.broadcasted_iota(jnp.int32, (6, width, 2, width), 1)
    j = lax.broadcasted_iota(jnp.int32, (6, width, 2, width), 2)
    z = lax.broadcasted_iota(jnp.int32, (6, width, 2, width), 3)
    dx = jnp.abs(i - j - 2)
    dy = jnp.abs(y - z)

    def line(distance, centre):
        return jnp.where(
            distance == 0, centre, jnp.where(distance == 1, 16.0, jnp.where(distance == 2, -1.0, 0.0))
        )

    value = jnp.where(dx == 0, line(dy, -60.0), jnp.where(dy == 0, line(dx, 0.0), 0.0))
    return value.reshape(6 * width, 2 * width).astype(jnp.bfloat16)


def cross_of(block, low, high, weights, diffusivity):
    owners, rows, variables, count, width = block.shape
    size = owners * count
    halo = pl.BlockSpec((owners, 2, 1, count, width), lambda v: (0, 0, v, 0, 0))
    return pl.pallas_call(
        cross_kernel,
        grid=(variables,),
        in_specs=[
            pl.BlockSpec((owners, rows, 1, count, width), lambda v: (0, 0, v, 0, 0)),
            halo,
            halo,
            pl.BlockSpec((rows, width), lambda v: (0, 0)),
            pl.BlockSpec((1, rows, width), lambda v: (v, 0, 0)),
            pl.BlockSpec((6 * width, 2 * width), lambda v: (0, 0)),
        ],
        out_specs=[
            pl.BlockSpec((size, size), lambda v: (0, 0)),
            pl.BlockSpec((2, 1, rows // 2, size, 2 * width), lambda v: (0, v, 0, 0, 0)),
        ],
        out_shape=[
            jax.ShapeDtypeStruct((size, size), jnp.float32),
            jax.ShapeDtypeStruct((2, variables, rows // 2, size, 2 * width), jnp.bfloat16),
        ],
        compiler_params=params(),
        cost_estimate=pl.CostEstimate(
            flops=10 * size * size * rows * variables * width,
            bytes_accessed=6 * size * rows * variables * width,
            transcendentals=0,
        ),
        name="cross",
    )(block, low, high, weights, diffusivity, band_matrix(width))


def modes_kernel(r_ref, f_ref, out_ref, turn_ref):
    pairs, size, width = f_ref.shape[2], f_ref.shape[3], f_ref.shape[4] // 2
    rows = 2 * pairs
    high, low = split(r_ref[...])
    for p in range(pairs):
        first, second = f_ref[0, 0, p], f_ref[1, 0, p]
        value = matmul(high, first) + matmul(high, second) + matmul(low, first)
        for k in range(2):
            turn_ref[pl.ds(2 * p + k, size, stride=rows), :] = value[:, k * width : (k + 1) * width]
    out_ref[:, 0] = turn_ref[...].reshape(size, rows, width).astype(out_ref.dtype)


def modes_of(rotation, field):
    _, variables, pairs, size, width = field.shape
    rows, width = 2 * pairs, width // 2
    return pl.pallas_call(
        modes_kernel,
        grid=(variables,),
        in_specs=[
            pl.BlockSpec((size, size), lambda v: (0, 0)),
            pl.BlockSpec((2, 1, pairs, size, 2 * width), lambda v: (0, v, 0, 0, 0)),
        ],
        out_specs=pl.BlockSpec((size, 1, rows, width), lambda v: (0, v, 0, 0)),
        out_shape=jax.ShapeDtypeStruct((size, variables, rows, width), jnp.bfloat16),
        scratch_shapes=[pltpu.VMEM((size * rows, width), jnp.float32)],
        compiler_params=params(),
        cost_estimate=pl.CostEstimate(
            flops=6 * size * size * rows * variables * width,
            bytes_accessed=6 * size * rows * variables * width,
            transcendentals=0,
        ),
        name="modes",
    )(rotation, field)


def summed(value, axis):
    count = lax.axis_size(axis)
    rows = value.shape[0] // count
    parts = value.reshape(count, rows, value.shape[1])
    own = jnp.sum(lax.all_to_all(parts, axis, 0, 0, tiled=True), axis=0, keepdims=True)
    every = lax.all_to_all(jnp.broadcast_to(own, parts.shape), axis, 0, 0, tiled=True)
    return every.reshape(value.shape)


def shifted(value, axis, step):
    count = lax.axis_size(axis)
    pairs = [(i, i + step) for i in range(count) if 0 <= i + step < count]
    return lax.ppermute(value, axis, pairs)


def make_rotation(gram_total):
    lower_factor = jnp.linalg.cholesky(gram_total)
    identity = jnp.eye(gram_total.shape[0], dtype=jnp.float32)
    return jax.scipy.linalg.solve_triangular(lower_factor, identity, lower=True)


def on_device(snapshots, cell_weights, diffusivity):
    highest = lax.Precision.HIGHEST
    owners = lax.axis_size("gx")
    block = lax.all_to_all(relayout(snapshots, owners), "gx", 0, 0, tiled=True)
    if snapshots.shape[0] % 16:
        count, rows, variables, each, width = block.shape
        block = block.transpose(1, 2, 0, 3, 4).reshape(1, rows, variables, count * each, width)
    rows, variables, width = block.shape[1], block.shape[2], block.shape[4]
    cell_count = rows * variables * width * owners
    gram_part = gram_of(block, cell_weights)
    low = shifted(block[:, rows - 2 :], "gx", 1)
    high = shifted(block[:, :2], "gx", -1)
    cross_part, field = cross_of(block, low, high, cell_weights, diffusivity)
    gram_total = summed(gram_part, "gx")
    cross_total = summed(cross_part, "gx") / cell_count
    rotation = make_rotation(gram_total / cell_count)
    reduced = jnp.dot(
        jnp.dot(rotation, cross_total, precision=highest), rotation.T, precision=highest
    )
    return (modes_of(rotation, field), reduced)


def solution(mesh):
    in_specs = (
        P("gx", None, "groups", None),
        P(("groups", "gx"), None),
        P(None, ("groups", "gx"), None),
    )
    out_specs = (P(None, None, ("groups", "gx"), None), P("groups", None))
    return jax.shard_map(
        on_device, mesh=mesh, in_specs=in_specs, out_specs=out_specs, check_vma=False
    )
```

```python
import jax
import jax.numpy as jnp
from jax import lax
from jax.experimental import pallas as pl
from jax.experimental.pallas import tpu as pltpu
from jax.sharding import PartitionSpec as P

VMEM_LIMIT = 48 * 1024 * 1024
NT = (((1,), (1,)), ((), ()))


def params():
    return pltpu.CompilerParams(vmem_limit_bytes=VMEM_LIMIT)


def split(value):
    high = value.astype(jnp.bfloat16)
    low = (value - high.astype(jnp.float32)).astype(jnp.bfloat16)
    return high, low


def matmul(a, b):
    return jnp.dot(a, b, preferred_element_type=jnp.float32)


def matmul_nt(a, b):
    return lax.dot_general(a, b, NT, preferred_element_type=jnp.float32)


def relayout_kernel(in_ref, out_ref):
    variables = in_ref.shape[1]
    for v in range(variables):
        block = in_ref[:, v].astype(jnp.float32)
        out_ref[0, :, v] = jnp.swapaxes(block, 0, 1).astype(out_ref.dtype)


def relayout(snapshots, owners):
    count, variables, cells, width = snapshots.shape
    rows = cells // owners
    if count % 16 or rows % 16:
        block = snapshots.reshape(count, variables, owners, rows, width)
        return block.transpose(2, 3, 1, 0, 4)
    return pl.pallas_call(
        relayout_kernel,
        grid=(owners,),
        in_specs=[pl.BlockSpec((count, variables, rows, width), lambda i: (0, 0, i, 0))],
        out_specs=pl.BlockSpec((1, rows, variables, count, width), lambda i: (i, 0, 0, 0, 0)),
        out_shape=jax.ShapeDtypeStruct((owners, rows, variables, count, width), snapshots.dtype),
        compiler_params=params(),
        name="relayout",
    )(snapshots)


def row_of(ref, x):
    value = ref[:, x, 0]
    return value.reshape(value.shape[0] * value.shape[1], value.shape[2])


def pack(gram):
    half = gram.shape[0] // 2
    sub = lax.broadcasted_iota(jnp.int32, (half, half), 0)
    lane = lax.broadcasted_iota(jnp.int32, (half, half), 1)
    first, last = gram[:half, :half], gram[half:, half:]
    diagonal = jnp.sum(jnp.where(lane == sub, first, 0.0), axis=0, keepdims=True)
    mixed = jnp.where(lane > sub, first, last)
    top = jnp.concatenate([mixed, gram[:half, half:]], axis=1)
    return top, jnp.broadcast_to(jnp.concatenate([diagonal, diagonal], axis=1), (16, 2 * half))


def unpack(mixed, diagonal):
    half = mixed.shape[0]
    sub = lax.broadcasted_iota(jnp.int32, (half, half), 0)
    lane = lax.broadcasted_iota(jnp.int32, (half, half), 1)
    upper = jnp.where(lane > sub, mixed, 0.0)
    lower = jnp.where(lane < sub, mixed, 0.0)
    first = jnp.where(lane == sub, diagonal, upper + upper.T)
    last = jnp.where(lane == sub, mixed, lower + lower.T)
    return first, last


def gram_kernel(x_ref, w_ref, out_ref, total_ref):
    rows = x_ref.shape[1]
    size = total_ref.shape[0]

    @pl.when(pl.program_id(0) == 0)
    def _():
        total_ref[...] = jnp.zeros_like(total_ref)

    total = None
    for first in range(0, rows, 4):
        group = range(first, first + 4)
        plain = jnp.concatenate([row_of(x_ref, x) for x in group], axis=1)
        weight = jnp.concatenate([w_ref[x : x + 1, :] for x in group], axis=1)
        high, low = split(plain.astype(jnp.float32) * weight)
        term = matmul_nt(high, plain) + matmul_nt(low, plain)
        total = term if total is None else total + term
    total_ref[...] += total

    @pl.when(pl.program_id(0) == pl.num_programs(0) - 1)
    def _():
        top, diagonal = pack(total_ref[...])
        out_ref[: size // 2, :] = top
        out_ref[size // 2 :, :] = diagonal


def gram_of(block, weights):
    owners, rows, variables, count, width = block.shape
    size = owners * count
    return pl.pallas_call(
        gram_kernel,
        grid=(variables,),
        in_specs=[
            pl.BlockSpec((owners, rows, 1, count, width), lambda v: (0, 0, v, 0, 0)),
            pl.BlockSpec((rows, width), lambda v: (0, 0)),
        ],
        out_specs=pl.BlockSpec((size // 2 + 16, size), lambda v: (0, 0)),
        out_shape=jax.ShapeDtypeStruct((size // 2 + 16, size), jnp.float32),
        scratch_shapes=[pltpu.VMEM((size, size), jnp.float32)],
        compiler_params=params(),
        cost_estimate=pl.CostEstimate(
            flops=4 * size * size * rows * variables * width,
            bytes_accessed=2 * size * rows * variables * width,
            transcendentals=0,
        ),
        name="gram",
    )(block, weights)


def cross_kernel(x_ref, low_ref, high_ref, w_ref, d_ref, band_ref, cross_ref, f_ref):
    rows = x_ref.shape[1]

    @pl.when(pl.program_id(0) == 0)
    def _():
        cross_ref[...] = jnp.zeros_like(cross_ref)

    def row(x):
        if x < 0:
            return row_of(low_ref, x + 2)
        if x >= rows:
            return row_of(high_ref, x - rows)
        return row_of(x_ref, x)

    total = None
    for x in range(0, rows, 2):
        near = jnp.concatenate([row(x + k) for k in range(-2, 4)], axis=1)
        plain = jnp.concatenate([row(x), row(x + 1)], axis=1)
        scale = jnp.concatenate([d_ref[0, x : x + 1, :], d_ref[0, x + 1 : x + 2, :]], axis=1)
        weight = jnp.concatenate([w_ref[x : x + 1, :], w_ref[x + 1 : x + 2, :]], axis=1)
        field = matmul(near, band_ref[...]) * (scale * (1.0 / 12.0))
        high, low = split(field)
        f_ref[0, 0, x // 2] = high
        f_ref[1, 0, x // 2] = low
        high, low = split(field * weight)
        term = matmul_nt(plain, high) + matmul_nt(plain, low)
        total = term if total is None else total + term
    cross_ref[...] += total


def band_matrix(width):
    i = lax.broadcasted_iota(jnp.int32, (6, width, 2, width), 0)
    y = lax.broadcasted_iota(jnp.int32, (6, width, 2, width), 1)
    j = lax.broadcasted_iota(jnp.int32, (6, width, 2, width), 2)
    z = lax.broadcasted_iota(jnp.int32, (6, width, 2, width), 3)
    dx = jnp.abs(i - j - 2)
    dy = jnp.abs(y - z)

    def line(distance, centre):
        return jnp.where(
            distance == 0, centre, jnp.where(distance == 1, 16.0, jnp.where(distance == 2, -1.0, 0.0))
        )

    value = jnp.where(dx == 0, line(dy, -60.0), jnp.where(dy == 0, line(dx, 0.0), 0.0))
    return value.reshape(6 * width, 2 * width).astype(jnp.bfloat16)


def cross_of(block, low, high, weights, diffusivity):
    owners, rows, variables, count, width = block.shape
    size = owners * count
    halo = pl.BlockSpec((owners, 2, 1, count, width), lambda v: (0, 0, v, 0, 0))
    return pl.pallas_call(
        cross_kernel,
        grid=(variables,),
        in_specs=[
            pl.BlockSpec((owners, rows, 1, count, width), lambda v: (0, 0, v, 0, 0)),
            halo,
            halo,
            pl.BlockSpec((rows, width), lambda v: (0, 0)),
            pl.BlockSpec((1, rows, width), lambda v: (v, 0, 0)),
            pl.BlockSpec((6 * width, 2 * width), lambda v: (0, 0)),
        ],
        out_specs=[
            pl.BlockSpec((size, size), lambda v: (0, 0)),
            pl.BlockSpec((2, 1, rows // 2, size, 2 * width), lambda v: (0, v, 0, 0, 0)),
        ],
        out_shape=[
            jax.ShapeDtypeStruct((size, size), jnp.float32),
            jax.ShapeDtypeStruct((2, variables, rows // 2, size, 2 * width), jnp.bfloat16),
        ],
        compiler_params=params(),
        cost_estimate=pl.CostEstimate(
            flops=10 * size * size * rows * variables * width,
            bytes_accessed=6 * size * rows * variables * width,
            transcendentals=0,
        ),
        name="cross",
    )(block, low, high, weights, diffusivity, band_matrix(width))


PANEL = 32
GROUP = 8


def lanes(value, width):
    return jnp.concatenate([value] * (width // value.shape[1]), axis=1)


def sublanes(value, height):
    return jnp.concatenate([value] * (height // value.shape[0]), axis=0)


def split3(value):
    high = value.astype(jnp.bfloat16)
    rest = value - high.astype(jnp.float32)
    middle = rest.astype(jnp.bfloat16)
    return high, middle, (rest - middle.astype(jnp.float32)).astype(jnp.bfloat16)


def eliminate(panel, start, at):
    height, size = panel.shape
    first = start + at
    sub = lax.broadcasted_iota(jnp.int32, (height, size), 0)
    lane = lax.broadcasted_iota(jnp.int32, (height, size), 1)
    sub1 = lax.broadcasted_iota(jnp.int32, (height, 128), 0)
    lane8 = lax.broadcasted_iota(jnp.int32, (8, size), 1)
    span = range(GROUP)
    columns = [jnp.broadcast_to(panel[:, first + i : first + i + 1], (height, 128)) for i in span]
    rows = [jnp.broadcast_to(panel[at + i : at + i + 1, :], (8, size)) for i in span]
    entry = {
        (i, k): jnp.broadcast_to(columns[k][at + i : at + i + 1, :], (8, 128))
        for i in span
        for k in range(i, GROUP)
    }
    inverse = []
    for i in span:
        inverse.append(1.0 / entry[i, i])
        rows[i] = jnp.where(lane8 == first + i, 1.0, rows[i])
        for k in range(i + 1, GROUP):
            factor = entry[i, k] * inverse[i]
            rows[k] = jnp.where(lane8 == first + i, 0.0, rows[k]) - lanes(factor, size) * rows[i]
            columns[k] = columns[k] - sublanes(factor, height) * columns[i]
            for j in range(i + 1, k + 1):
                entry[j, k] = entry[j, k] - factor * entry[i, j]
    rows = [
        jnp.where((lane8 > first + i) & (lane8 < first + GROUP), 0.0, rows[i]) for i in span
    ]
    done = at + GROUP
    result = jnp.where((lane >= first) & (lane < first + GROUP) & (sub >= done), 0.0, panel)
    for i in span:
        factor = jnp.where(sub1 >= done, columns[i] * sublanes(inverse[i], height), 0.0)
        result = result - lanes(factor, size) * sublanes(rows[i], height)
    for i in span:
        result = jnp.where(sub == at + i, sublanes(rows[i], height), result)
    return result, [entry[i, i] for i in span]


def rotation_kernel(scale, gram_ref, out_ref, work_ref):
    size = out_ref.shape[0]
    half = size // 2
    first, last = unpack(gram_ref[:half, :half] * scale, gram_ref[half : half + 1, :half] * scale)
    work_ref[:half, :half] = first
    work_ref[half:, half:] = last
    work_ref[:half, half:] = gram_ref[:half, half:] * scale
    work_ref[half:, :half] = jnp.zeros((half, half), jnp.float32)
    sub = lax.broadcasted_iota(jnp.int32, (PANEL, size), 0)
    lane = lax.broadcasted_iota(jnp.int32, (PANEL, size), 1)
    sub1 = lax.broadcasted_iota(jnp.int32, (PANEL, 128), 0)
    for start in range(0, size, PANEL):
        end = start + PANEL
        panel = work_ref[start:end, :]
        norm = jnp.zeros((PANEL, 128), jnp.float32)
        for at in range(0, PANEL, GROUP):
            panel, pivots = eliminate(panel, start, at)
            for i, pivot in enumerate(pivots):
                norm = jnp.where(sub1 == at + i, sublanes(lax.rsqrt(pivot), PANEL), norm)
        panel = panel * lanes(norm, size)
        panel = jnp.where((lane > start + sub) & (lane < end), 0.0, panel)
        out_ref[start:end, :] = jnp.where(lane < end, panel, 0.0)
        if end < size:
            high, middle, low = split3(panel)
            right = jnp.concatenate([high, middle, low, high, middle, high], axis=0)
            left = jnp.concatenate(
                [part[:, end:] for part in (high, high, high, middle, middle, low)], axis=0
            )
            update = lax.dot_general(
                left, right, (((0,), (0,)), ((), ())), preferred_element_type=jnp.float32
            )
            rest = work_ref[end:, :]
            place = lax.broadcasted_iota(jnp.int32, rest.shape, 1)
            work_ref[end:, :] = jnp.where((place >= start) & (place < end), 0.0, rest) - update


def rotation_of(packed, cell_count):
    size = packed.shape[1]
    return pl.pallas_call(
        lambda *refs: rotation_kernel(1.0 / cell_count, *refs),
        out_shape=jax.ShapeDtypeStruct((size, size), jnp.float32),
        scratch_shapes=[pltpu.VMEM((size, size), jnp.float32)],
        compiler_params=params(),
        cost_estimate=pl.CostEstimate(
            flops=1 << 33, bytes_accessed=8 * size * size, transcendentals=0
        ),
        name="rotation",
    )(packed)


def modes_kernel(r_ref, f_ref, out_ref, turn_ref):
    pairs, size, width = f_ref.shape[2], f_ref.shape[3], f_ref.shape[4] // 2
    rows = 2 * pairs
    high, low = split(r_ref[...])
    for p in range(pairs):
        first, second = f_ref[0, 0, p], f_ref[1, 0, p]
        value = matmul(high, first) + matmul(high, second) + matmul(low, first)
        for k in range(2):
            turn_ref[pl.ds(2 * p + k, size, stride=rows), :] = value[:, k * width : (k + 1) * width]
    out_ref[:, 0] = turn_ref[...].reshape(size, rows, width).astype(out_ref.dtype)


def modes_of(rotation, field):
    _, variables, pairs, size, width = field.shape
    rows, width = 2 * pairs, width // 2
    return pl.pallas_call(
        modes_kernel,
        grid=(variables,),
        in_specs=[
            pl.BlockSpec((size, size), lambda v: (0, 0)),
            pl.BlockSpec((2, 1, pairs, size, 2 * width), lambda v: (0, v, 0, 0, 0)),
        ],
        out_specs=pl.BlockSpec((size, 1, rows, width), lambda v: (0, v, 0, 0)),
        out_shape=jax.ShapeDtypeStruct((size, variables, rows, width), jnp.bfloat16),
        scratch_shapes=[pltpu.VMEM((size * rows, width), jnp.float32)],
        compiler_params=params(),
        cost_estimate=pl.CostEstimate(
            flops=6 * size * size * rows * variables * width,
            bytes_accessed=6 * size * rows * variables * width,
            transcendentals=0,
        ),
        name="modes",
    )(rotation, field)


def summed(value, axis):
    count = lax.axis_size(axis)
    if count & (count - 1) or count < 2:
        return lax.psum(value, axis)
    half = value.shape[0] // 2
    odd = lax.axis_index(axis) % 2 == 1
    first, second = value[:half], value[half:]

    def swap(part, step):
        return lax.ppermute(part, axis, [(i, i ^ step) for i in range(count)])

    own = jnp.where(odd, second, first) + swap(jnp.where(odd, first, second), 1)
    step = 2
    while step < count:
        own = own + swap(own, step)
        step *= 2
    other = swap(own, 1)
    return jnp.concatenate([jnp.where(odd, other, own), jnp.where(odd, own, other)], axis=0)


def shifted(value, axis, step):
    count = lax.axis_size(axis)
    pairs = [(i, i + step) for i in range(count) if 0 <= i + step < count]
    return lax.ppermute(value, axis, pairs)


def on_device(snapshots, cell_weights, diffusivity):
    highest = lax.Precision.HIGHEST
    owners = lax.axis_size("gx")
    block = lax.all_to_all(relayout(snapshots, owners), "gx", 0, 0, tiled=True)
    if snapshots.shape[0] % 16:
        count, rows, variables, each, width = block.shape
        block = block.transpose(1, 2, 0, 3, 4).reshape(1, rows, variables, count * each, width)
    rows, variables, width = block.shape[1], block.shape[2], block.shape[4]
    cell_count = rows * variables * width * owners
    gram_part = gram_of(block, cell_weights)
    low = shifted(block[:, rows - 2 :], "gx", 1)
    high = shifted(block[:, :2], "gx", -1)
    cross_part, field = cross_of(block, low, high, cell_weights, diffusivity)
    gram_total = summed(gram_part, "gx")
    cross_total = summed(cross_part, "gx") / cell_count
    rotation = rotation_of(gram_total, cell_count)
    reduced = jnp.dot(
        jnp.dot(rotation, cross_total, precision=highest), rotation.T, precision=highest
    )
    return (modes_of(rotation, field), reduced)


def solution(mesh):
    in_specs = (
        P("gx", None, "groups", None),
        P(("groups", "gx"), None),
        P(None, ("groups", "gx"), None),
    )
    out_specs = (P(None, None, ("groups", "gx"), None), P("groups", None))
    return jax.shard_map(
        on_device, mesh=mesh, in_specs=in_specs, out_specs=out_specs, check_vma=False
    )
```

```python
import functools

import jax
import jax.numpy as jnp
from jax import lax
from jax.experimental import pallas as pl
from jax.experimental.pallas import tpu as pltpu
from jax.sharding import PartitionSpec as P

VMEM_LIMIT = 24 * 1024 * 1024
NT = (((1,), (1,)), ((), ()))


def params():
    return pltpu.CompilerParams(vmem_limit_bytes=VMEM_LIMIT)


def split(value):
    high = value.astype(jnp.bfloat16)
    low = (value - high.astype(jnp.float32)).astype(jnp.bfloat16)
    return high, low


def matmul(a, b):
    return jnp.dot(a, b, preferred_element_type=jnp.float32)


def matmul_nt(a, b):
    return lax.dot_general(a, b, NT, preferred_element_type=jnp.float32)


def relayout_kernel(in_ref, out_ref):
    owners, rows, variables = out_ref.shape[:3]
    for owner in range(owners):
        for v in range(variables):
            block = in_ref[:, v, owner * rows : (owner + 1) * rows]
            out_ref[owner, :, v] = jnp.swapaxes(block, 0, 1)


def relayout(snapshots, owners):
    count, variables, cells, width = snapshots.shape
    rows = cells // owners
    if count % 16 or rows % 16:
        block = snapshots.reshape(count, variables, owners, rows, width)
        return block.transpose(2, 3, 1, 0, 4)
    each = owners // 2 if owners % 2 == 0 else 1
    return pl.pallas_call(
        relayout_kernel,
        grid=(owners // each,),
        in_specs=[pl.BlockSpec((count, variables, each * rows, width), lambda i: (0, 0, i, 0))],
        out_specs=pl.BlockSpec(
            (each, rows, variables, count, width), lambda i: (i, 0, 0, 0, 0)
        ),
        out_shape=jax.ShapeDtypeStruct((owners, rows, variables, count, width), snapshots.dtype),
        compiler_params=pltpu.CompilerParams(vmem_limit_bytes=60 * 1024 * 1024),
        name="relayout",
    )(snapshots)


def row_of(ref, x, v):
    value = ref[:, x, v]
    return value.reshape(value.shape[0] * value.shape[1], value.shape[2])


def pack(gram):
    half = gram.shape[0] // 2
    sub = lax.broadcasted_iota(jnp.int32, (half, half), 0)
    lane = lax.broadcasted_iota(jnp.int32, (half, half), 1)
    first, last = gram[:half, :half], gram[half:, half:]
    diagonal = jnp.sum(jnp.where(lane == sub, first, 0.0), axis=0, keepdims=True)
    mixed = jnp.where(lane > sub, first, last)
    top = jnp.concatenate([mixed, gram[:half, half:]], axis=1)
    return top, jnp.broadcast_to(jnp.concatenate([diagonal, diagonal], axis=1), (16, 2 * half))


def unpack(mixed, diagonal):
    half = mixed.shape[0]
    sub = lax.broadcasted_iota(jnp.int32, (half, half), 0)
    lane = lax.broadcasted_iota(jnp.int32, (half, half), 1)
    upper = jnp.where(lane > sub, mixed, 0.0)
    lower = jnp.where(lane < sub, mixed, 0.0)
    first = jnp.where(lane == sub, diagonal, upper + upper.T)
    last = jnp.where(lane == sub, mixed, lower + lower.T)
    return first, last


def gram_kernel(x_ref, w_ref, out_ref, total_ref):
    rows = x_ref.shape[1]
    size = total_ref.shape[0]

    @pl.when(pl.program_id(0) == 0)
    def _():
        total_ref[...] = jnp.zeros_like(total_ref)

    total = None
    for v in range(x_ref.shape[2]):
        for first in range(0, rows, 4):
            group = range(first, first + 4)
            plain = jnp.concatenate([row_of(x_ref, x, v) for x in group], axis=1)
            weight = jnp.concatenate([w_ref[x : x + 1, :] for x in group], axis=1)
            high, low = split(plain.astype(jnp.float32) * weight)
            term = matmul_nt(high, plain) + matmul_nt(low, plain)
            total = term if total is None else total + term
    total_ref[...] += total

    @pl.when(pl.program_id(0) == pl.num_programs(0) - 1)
    def _():
        top, diagonal = pack(total_ref[...])
        out_ref[: size // 2, :] = top
        out_ref[size // 2 :, :] = diagonal


def gram_of(block, weights):
    owners, rows, variables, count, width = block.shape
    size = owners * count
    each = 2 if variables % 2 == 0 else 1
    return pl.pallas_call(
        gram_kernel,
        grid=(variables // each,),
        in_specs=[
            pl.BlockSpec((owners, rows, each, count, width), lambda v: (0, 0, v, 0, 0)),
            pl.BlockSpec((rows, width), lambda v: (0, 0)),
        ],
        out_specs=pl.BlockSpec((size // 2 + 16, size), lambda v: (0, 0)),
        out_shape=jax.ShapeDtypeStruct((size // 2 + 16, size), jnp.float32),
        scratch_shapes=[pltpu.VMEM((size, size), jnp.float32)],
        compiler_params=params(),
        cost_estimate=pl.CostEstimate(
            flops=4 * size * size * rows * variables * width,
            bytes_accessed=2 * size * rows * variables * width,
            transcendentals=0,
        ),
        name="gram",
    )(block, weights)


def cross_kernel(span, odd_ref, x_ref, near_ref, far_ref, w_ref, d_ref, band_ref, cross_ref, f_ref):
    rows = x_ref.shape[1]
    odd = odd_ref[0] == 1
    cross_ref[...] = jnp.zeros_like(cross_ref)
    for place, v in enumerate(span):
        plain = [row_of(x_ref, x, v) for x in range(rows)]
        near = [row_of(near_ref, x, v) for x in range(2)]
        far = [row_of(far_ref, x, v) for x in range(2)]
        below = [jnp.where(odd, near[x], far[x]) for x in range(2)]
        above = [jnp.where(odd, far[x], near[x]) for x in range(2)]
        value = [part.astype(jnp.float32) for part in below + plain + above]
        total = None
        for x in range(0, rows, 2):
            pair = jnp.concatenate(plain[x : x + 2], axis=1)
            along_x = [
                16.0 * (value[k + 1] + value[k + 3]) - (value[k] + value[k + 4])
                for k in (x, x + 1)
            ]
            scale = jnp.concatenate([d_ref[v, x : x + 1, :], d_ref[v, x + 1 : x + 2, :]], axis=1)
            weight = jnp.concatenate([w_ref[x : x + 1, :], w_ref[x + 1 : x + 2, :]], axis=1)
            both = matmul(pair, band_ref[...]) + jnp.concatenate(along_x, axis=1)
            field = both * (scale * (1.0 / 12.0))
            high, low = split(field)
            f_ref[0, place, x // 2] = high
            f_ref[1, place, x // 2] = low
            term = matmul_nt(jnp.concatenate(split(field * weight), axis=0), pair)
            term = term[: term.shape[0] // 2] + term[term.shape[0] // 2 :]
            total = term if total is None else total + term
        cross_ref[...] += total


def band_matrix(width):
    shape = (2, width, 2, width)
    i, y, j, z = (lax.broadcasted_iota(jnp.int32, shape, axis) for axis in range(4))
    distance = jnp.abs(y - z)
    line = jnp.where(
        distance == 0, -60.0, jnp.where(distance == 1, 16.0, jnp.where(distance == 2, -1.0, 0.0))
    )
    return jnp.where(i == j, line, 0.0).reshape(2 * width, 2 * width).astype(jnp.bfloat16)


def cross_of(span, odd, block, near, far, weights, diffusivity, band):
    owners, rows, variables, count, width = block.shape
    size = owners * count
    vmem = pl.BlockSpec(memory_space=pltpu.VMEM)
    return pl.pallas_call(
        lambda *refs: cross_kernel(span, *refs),
        in_specs=[pl.BlockSpec(memory_space=pltpu.SMEM)] + [vmem] * 6,
        out_specs=[vmem, vmem],
        out_shape=[
            jax.ShapeDtypeStruct((size, size), jnp.float32),
            jax.ShapeDtypeStruct((2, len(span), rows // 2, size, 2 * width), jnp.bfloat16),
        ],
        compiler_params=params(),
        cost_estimate=pl.CostEstimate(
            flops=12 * size * size * rows * len(span) * width,
            bytes_accessed=6 * size * rows * len(span) * width,
            transcendentals=0,
        ),
        name="cross",
    )(odd, block, near, far, weights, diffusivity, band)


PANEL = 32
GROUP = 8


def lanes(value, width):
    return jnp.concatenate([value] * (width // value.shape[1]), axis=1)


def sublanes(value, height):
    return jnp.concatenate([value] * (height // value.shape[0]), axis=0)


def split3(value):
    high = value.astype(jnp.bfloat16)
    rest = value - high.astype(jnp.float32)
    middle = rest.astype(jnp.bfloat16)
    return high, middle, (rest - middle.astype(jnp.float32)).astype(jnp.bfloat16)


def eliminate(panel, start, at):
    height, size = panel.shape
    first = start + at
    sub = lax.broadcasted_iota(jnp.int32, (height, size), 0)
    lane = lax.broadcasted_iota(jnp.int32, (height, size), 1)
    sub1 = lax.broadcasted_iota(jnp.int32, (height, 128), 0)
    lane8 = lax.broadcasted_iota(jnp.int32, (8, size), 1)
    span = range(GROUP)
    columns = [jnp.broadcast_to(panel[:, first + i : first + i + 1], (height, 128)) for i in span]
    rows = [jnp.broadcast_to(panel[at + i : at + i + 1, :], (8, size)) for i in span]
    entry = {
        (i, k): jnp.broadcast_to(columns[k][at + i : at + i + 1, :], (8, 128))
        for i in span
        for k in range(i, GROUP)
    }
    inverse = []
    for i in span:
        inverse.append(1.0 / entry[i, i])
        rows[i] = jnp.where(lane8 == first + i, 1.0, rows[i])
        for k in range(i + 1, GROUP):
            factor = entry[i, k] * inverse[i]
            rows[k] = jnp.where(lane8 == first + i, 0.0, rows[k]) - lanes(factor, size) * rows[i]
            columns[k] = columns[k] - sublanes(factor, height) * columns[i]
            for j in range(i + 1, k + 1):
                entry[j, k] = entry[j, k] - factor * entry[i, j]
    rows = [
        jnp.where((lane8 > first + i) & (lane8 < first + GROUP), 0.0, rows[i]) for i in span
    ]
    done = at + GROUP
    result = jnp.where((lane >= first) & (lane < first + GROUP) & (sub >= done), 0.0, panel)
    for i in span:
        factor = jnp.where(sub1 >= done, columns[i] * sublanes(inverse[i], height), 0.0)
        result = result - lanes(factor, size) * sublanes(rows[i], height)
    for i in span:
        result = jnp.where(sub == at + i, sublanes(rows[i], height), result)
    return result, [entry[i, i] for i in span]


def rotation_kernel(scale, gram_ref, out_ref, work_ref):
    size = out_ref.shape[0]
    half = size // 2
    first, last = unpack(gram_ref[:half, :half] * scale, gram_ref[half : half + 1, :half] * scale)
    work_ref[:half, :half] = first
    work_ref[half:, half:] = last
    work_ref[:half, half:] = gram_ref[:half, half:] * scale
    work_ref[half:, :half] = jnp.zeros((half, half), jnp.float32)
    sub = lax.broadcasted_iota(jnp.int32, (PANEL, size), 0)
    lane = lax.broadcasted_iota(jnp.int32, (PANEL, size), 1)
    sub1 = lax.broadcasted_iota(jnp.int32, (PANEL, 128), 0)
    for start in range(0, size, PANEL):
        end = start + PANEL
        panel = work_ref[start:end, :]
        norm = jnp.zeros((PANEL, 128), jnp.float32)
        for at in range(0, PANEL, GROUP):
            panel, pivots = eliminate(panel, start, at)
            for i, pivot in enumerate(pivots):
                norm = jnp.where(sub1 == at + i, sublanes(lax.rsqrt(pivot), PANEL), norm)
        panel = panel * lanes(norm, size)
        panel = jnp.where((lane > start + sub) & (lane < end), 0.0, panel)
        out_ref[start:end, :] = jnp.where(lane < end, panel, 0.0)
        if end < size:
            high, middle, low = split3(panel)
            right = jnp.concatenate([high, middle, low, high, middle, high], axis=0)
            left = jnp.concatenate(
                [part[:, end:] for part in (high, high, high, middle, middle, low)], axis=0
            )
            update = lax.dot_general(
                left, right, (((0,), (0,)), ((), ())), preferred_element_type=jnp.float32
            )
            rest = work_ref[end:, :]
            place = lax.broadcasted_iota(jnp.int32, rest.shape, 1)
            work_ref[end:, :] = jnp.where((place >= start) & (place < end), 0.0, rest) - update


def rotation_of(packed, cell_count):
    size = packed.shape[1]
    return pl.pallas_call(
        lambda *refs: rotation_kernel(1.0 / cell_count, *refs),
        out_shape=jax.ShapeDtypeStruct((size, size), jnp.float32),
        scratch_shapes=[pltpu.VMEM((size, size), jnp.float32)],
        compiler_params=params(),
        cost_estimate=pl.CostEstimate(
            flops=1 << 33, bytes_accessed=8 * size * size, transcendentals=0
        ),
        name="rotation",
    )(packed)


def modes_kernel(r_ref, *refs):
    fields, out_ref = refs[:-1], refs[-1]
    high, low = split(r_ref[...])
    at = pl.program_id(0)

    def store(field, v):
        width = field.shape[4] // 2
        rows = []
        for p in range(field.shape[2]):
            first, second = field[0, v, p], field[1, v, p]
            value = matmul(high, first) + matmul(high, second) + matmul(low, first)
            value = value.astype(out_ref.dtype)
            rows += [value[:, :width], value[:, width:]]
        out_ref[:, 0] = jnp.swapaxes(jnp.stack(rows, axis=0), 0, 1)

    first = 0
    for field in fields:
        last = first + field.shape[1]
        pl.when((at >= first) & (at < last))(functools.partial(store, field, at - first))
        first = last


def modes_of(rotation, fields):
    _, _, pairs, size, width = fields[0].shape
    variables = sum(field.shape[1] for field in fields)
    rows, width = 2 * pairs, width // 2
    vmem = pl.BlockSpec(memory_space=pltpu.VMEM)
    return pl.pallas_call(
        modes_kernel,
        grid=(variables,),
        in_specs=[pl.BlockSpec((size, size), lambda v: (0, 0))] + [vmem] * len(fields),
        out_specs=pl.BlockSpec((size, 1, rows, width), lambda v: (0, v, 0, 0)),
        out_shape=jax.ShapeDtypeStruct((size, variables, rows, width), jnp.bfloat16),
        compiler_params=params(),
        cost_estimate=pl.CostEstimate(
            flops=10 * size * size * rows * variables * width,
            bytes_accessed=6 * size * rows * variables * width,
            transcendentals=0,
        ),
        name="modes",
    )(rotation, *fields)


def summed(value, axis):
    count = lax.axis_size(axis)
    if count & (count - 1) or count < 2:
        return lax.psum(value, axis)
    half = value.shape[0] // 2
    odd = lax.axis_index(axis) % 2 == 1
    first, second = value[:half], value[half:]

    def swap(part, step):
        return lax.ppermute(part, axis, [(i, i ^ step) for i in range(count)])

    own = jnp.where(odd, second, first) + swap(jnp.where(odd, first, second), 1)
    step = 2
    while step < count:
        own = own + swap(own, step)
        step *= 2
    other = swap(own, 1)
    return jnp.concatenate([jnp.where(odd, other, own), jnp.where(odd, own, other)], axis=0)


def edges(block, axis):
    count = lax.axis_size(axis)
    rows = block.shape[1]
    odd = lax.axis_index(axis) % 2 == 1
    received = []
    for start, first in ((jnp.where(odd, 0, rows - 2), 0), (jnp.where(odd, rows - 2, 0), 1)):
        part = lax.dynamic_slice_in_dim(block, start, 2, axis=1)
        pairs = [(i, i + 1) for i in range(first, count - 1, 2)]
        received.append(lax.ppermute(part, axis, pairs + [(b, a) for a, b in pairs]))
    return received


def on_device(snapshots, cell_weights, diffusivity):
    highest = lax.Precision.HIGHEST
    owners = lax.axis_size("gx")
    block = lax.all_to_all(relayout(snapshots, owners), "gx", 0, 0, tiled=True)
    if snapshots.shape[0] % 16:
        count, rows, variables, each, width = block.shape
        block = block.transpose(1, 2, 0, 3, 4).reshape(1, rows, variables, count * each, width)
    rows, variables, width = block.shape[1], block.shape[2], block.shape[4]
    cell_count = rows * variables * width * owners
    near, far = edges(block, "gx")
    gram_part = gram_of(block, cell_weights)
    odd = (lax.axis_index("gx") % 2).astype(jnp.int32).reshape(1)
    band = band_matrix(width)
    half = variables // 2
    crosses, fields = zip(
        *(
            cross_of(span, odd, block, near, far, cell_weights, diffusivity, band)
            for span in (range(half), range(half, variables))
            if len(span)
        )
    )
    gram_total = summed(gram_part, "gx")
    cross_total = summed(sum(crosses[1:], crosses[0]), "gx") * (1.0 / cell_count)
    rotation = rotation_of(gram_total, cell_count)
    reduced = jnp.dot(
        jnp.dot(rotation, cross_total.T, precision=highest), rotation.T, precision=highest
    )
    return (modes_of(rotation, fields), reduced)


def solution(mesh):
    in_specs = (
        P("gx", None, "groups", None),
        P(("groups", "gx"), None),
        P(None, ("groups", "gx"), None),
    )
    out_specs = (P(None, None, ("groups", "gx"), None), P("groups", None))
    return jax.shard_map(
        on_device, mesh=mesh, in_specs=in_specs, out_specs=out_specs, check_vma=False
    )
```

```python
import functools

import jax
import jax.numpy as jnp
from jax import lax
from jax.experimental import pallas as pl
from jax.experimental.pallas import tpu as pltpu
from jax.sharding import PartitionSpec as P

VMEM_LIMIT = 24 * 1024 * 1024
NT = (((1,), (1,)), ((), ()))


def cost(flops):
    return pl.CostEstimate(flops=int(flops), bytes_accessed=1, transcendentals=0)


VMEM = pl.BlockSpec(memory_space=pltpu.VMEM)


def params():
    return pltpu.CompilerParams(vmem_limit_bytes=VMEM_LIMIT)


def split(value):
    high = value.astype(jnp.bfloat16)
    low = (value - high.astype(jnp.float32)).astype(jnp.bfloat16)
    return high, low


def matmul(a, b):
    return jnp.dot(a, b, preferred_element_type=jnp.float32)


def matmul_nt(a, b):
    return lax.dot_general(a, b, NT, preferred_element_type=jnp.float32)


def relayout_kernel(in_ref, out_ref):
    owners, rows, variables = out_ref.shape[:3]
    for owner in range(owners):
        for v in range(variables):
            block = in_ref[:, v, owner * rows : (owner + 1) * rows]
            out_ref[owner, :, v] = jnp.swapaxes(block, 0, 1)


def relayout(snapshots, owners):
    count, variables, cells, width = snapshots.shape
    rows = cells // owners
    if count % 16 or rows % 16:
        block = snapshots.reshape(count, variables, owners, rows, width)
        return block.transpose(2, 3, 1, 0, 4)
    each = owners // 2 if owners % 2 == 0 else 1
    return pl.pallas_call(
        relayout_kernel,
        grid=(owners // each,),
        in_specs=[pl.BlockSpec((count, variables, each * rows, width), lambda i: (0, 0, i, 0))],
        out_specs=pl.BlockSpec(
            (each, rows, variables, count, width), lambda i: (i, 0, 0, 0, 0)
        ),
        out_shape=jax.ShapeDtypeStruct((owners, rows, variables, count, width), snapshots.dtype),
        compiler_params=pltpu.CompilerParams(vmem_limit_bytes=60 * 1024 * 1024),
        name="relayout",
    )(snapshots)


def row_of(ref, x, v):
    value = ref[:, x, v]
    return value.reshape(value.shape[0] * value.shape[1], value.shape[2])


def pack(gram):
    half = gram.shape[0] // 2
    sub = lax.broadcasted_iota(jnp.int32, (half, half), 0)
    lane = lax.broadcasted_iota(jnp.int32, (half, half), 1)
    first, last = gram[:half, :half], gram[half:, half:]
    diagonal = jnp.sum(jnp.where(lane == sub, first, 0.0), axis=0, keepdims=True)
    mixed = jnp.where(lane > sub, first, last)
    top = jnp.concatenate([mixed, gram[:half, half:]], axis=1)
    return top, jnp.broadcast_to(jnp.concatenate([diagonal, diagonal], axis=1), (16, 2 * half))


def unpack(mixed, diagonal):
    half = mixed.shape[0]
    sub = lax.broadcasted_iota(jnp.int32, (half, half), 0)
    lane = lax.broadcasted_iota(jnp.int32, (half, half), 1)
    upper = jnp.where(lane > sub, mixed, 0.0)
    lower = jnp.where(lane < sub, mixed, 0.0)
    first = jnp.where(lane == sub, diagonal, upper + upper.T)
    last = jnp.where(lane == sub, mixed, lower + lower.T)
    return first, last


def gram_kernel(x_ref, w_ref, out_ref, keep_ref, total_ref):
    rows, each = x_ref.shape[1:3]
    size = total_ref.shape[0]

    @pl.when(pl.program_id(0) == 0)
    def _():
        total_ref[...] = jnp.zeros_like(total_ref)

    total = None
    for v in range(each):
        for first in range(0, rows, 4):
            group = range(first, first + 4)
            plain = [row_of(x_ref, x, v) for x in group]
            at = pl.program_id(0) * each + v
            for x in group:
                keep_ref[at, x] = plain[x - first]
            plain = jnp.concatenate(plain, axis=1)
            weight = jnp.concatenate([w_ref[x : x + 1, :] for x in group], axis=1)
            high, low = split(plain.astype(jnp.float32) * weight)
            term = matmul_nt(high, plain) + matmul_nt(low, plain)
            total = term if total is None else total + term
    total_ref[...] += total

    @pl.when(pl.program_id(0) == pl.num_programs(0) - 1)
    def _():
        top, diagonal = pack(total_ref[...])
        out_ref[: size // 2, :] = top
        out_ref[size // 2 :, :] = diagonal


def gram_of(block, weights):
    owners, rows, variables, count, width = block.shape
    size = owners * count
    each = 2 if variables % 2 == 0 else 1
    return pl.pallas_call(
        gram_kernel,
        grid=(variables // each,),
        in_specs=[
            pl.BlockSpec((owners, rows, each, count, width), lambda v: (0, 0, v, 0, 0)),
            pl.BlockSpec((rows, width), lambda v: (0, 0)),
        ],
        out_specs=[pl.BlockSpec((size // 2 + 16, size), lambda v: (0, 0)), VMEM],
        out_shape=[
            jax.ShapeDtypeStruct((size // 2 + 16, size), jnp.float32),
            jax.ShapeDtypeStruct((variables, rows, size, width), block.dtype),
        ],
        scratch_shapes=[pltpu.VMEM((size, size), jnp.float32)],
        compiler_params=params(),
        cost_estimate=cost(2e9),
        name="gram",
    )(block, weights)


def along_x(lower, upper, centre):
    near = [part for part in (lower[1], upper[0]) if part is not None]
    far = [part for part in (lower[0], upper[1]) if part is not None]
    value = 16.0 * sum(near[1:], near[0]) if near else jnp.zeros_like(centre)
    return value - sum(far[1:], far[0]) if far else value


def two(ref, x):
    return jnp.concatenate([ref[x : x + 1, :], ref[x + 1 : x + 2, :]], axis=1)


def stencil(value, x, pair, d_ref, band_ref):
    sides = [
        along_x((value.get(k - 2), value.get(k - 1)), (value.get(k + 1), value.get(k + 2)), value[k])
        for k in (x, x + 1)
    ]
    both = matmul(pair, band_ref[...]) + jnp.concatenate(sides, axis=1)
    return both * (two(d_ref, x) * (1.0 / 12.0))


def products(left, right):
    term = matmul_nt(jnp.concatenate(split(left), axis=0), right)
    half = term.shape[0] // 2
    return term[:half] + term[half:]


def store(f_ref, v, p, field):
    f_ref[0, v, p], f_ref[1, v, p] = split(field)


def inner_kernel(span, x_ref, w_ref, d_ref, band_ref, before_ref, cross_ref, f_ref):
    rows = x_ref.shape[1]
    cross_ref[...] = before_ref[...]
    for place, v in enumerate(span):
        plain = [x_ref[v, x] for x in range(rows)]
        value = {x: part.astype(jnp.float32) for x, part in enumerate(plain)}
        total = None
        for x in range(2, rows, 2):
            pair = jnp.concatenate(plain[x : x + 2], axis=1)
            field = stencil(value, x, pair, d_ref.at[v], band_ref)
            if x < rows - 2:
                store(f_ref, place, x // 2 - 1, field)
            term = products(field * two(w_ref, x), pair)
            total = term if total is None else total + term
        cross_ref[...] += total


def lower_kernel(odd_ref, x_ref, near_ref, far_ref, w_ref, d_ref, band_ref, before_ref, cross_ref, f_ref):
    variables, owners = x_ref.shape[0], near_ref.shape[0] - 1
    odd = odd_ref[0] == 1
    cross_ref[...] = before_ref[...]
    for v in range(variables):
        plain = {x: x_ref[v, x] for x in range(4)}
        for x in range(2):
            near, far = (row_of(ref.at[:owners], x, v) for ref in (near_ref, far_ref))
            plain[x - 2] = jnp.where(odd, near, far)
        value = {x: part.astype(jnp.float32) for x, part in plain.items()}
        pair = jnp.concatenate([plain[0], plain[1]], axis=1)
        field = stencil(value, 0, pair, d_ref.at[v], band_ref)
        store(f_ref, v, 0, field)
        total = products(field * two(w_ref, 0), pair)
        factor = []
        for x in range(2):
            near, far = (ref[owners, x, v].astype(jnp.float32) for ref in (near_ref, far_ref))
            parts = jnp.where(odd, near, far)
            factor.append(parts[0:1] + parts[1:2] + parts[2:3])
        joined = jnp.concatenate(
            [-value[0] * factor[0], (16.0 * value[0] - value[1]) * factor[1]], axis=1
        )
        total = total + products(joined, jnp.concatenate([plain[-2], plain[-1]], axis=1))
        cross_ref[...] += total


def upper_kernel(odd_ref, x_ref, near_ref, far_ref, d_ref, band_ref, f_ref):
    variables, rows = x_ref.shape[:2]
    owners = near_ref.shape[0] - 1
    odd = odd_ref[0] == 1
    for v in range(variables):
        plain = {x: x_ref[v, x] for x in range(rows - 4, rows)}
        for x in range(2):
            near, far = (row_of(ref.at[:owners], x, v) for ref in (near_ref, far_ref))
            plain[rows + x] = jnp.where(odd, far, near)
        value = {x: part.astype(jnp.float32) for x, part in plain.items()}
        pair = jnp.concatenate([plain[rows - 2], plain[rows - 1]], axis=1)
        store(f_ref, v, 0, stencil(value, rows - 2, pair, d_ref.at[v], band_ref))


def band_matrix(width):
    shape = (2, width, 2, width)
    i, y, j, z = (lax.broadcasted_iota(jnp.int32, shape, axis) for axis in range(4))
    distance = jnp.abs(y - z)
    line = jnp.where(
        distance == 0, -60.0, jnp.where(distance == 1, 16.0, jnp.where(distance == 2, -1.0, 0.0))
    )
    return jnp.where(i == j, line, 0.0).reshape(2 * width, 2 * width).astype(jnp.bfloat16)


COST = {"inner": 1, "lower": 1, "upper": 1}


def stencil_call(kernel, name, block, span, pairs, cross, *operands, odd=None):
    _, _, size, width = block.shape
    field = jax.ShapeDtypeStruct((2, span, pairs, size, 2 * width), jnp.bfloat16)
    total = jax.ShapeDtypeStruct((size, size), jnp.float32)
    flags = [] if odd is None else [odd]
    return pl.pallas_call(
        kernel,
        in_specs=[pl.BlockSpec(memory_space=pltpu.SMEM)] * len(flags) + [VMEM] * (1 + len(operands)),
        out_specs=[VMEM, VMEM] if cross else VMEM,
        out_shape=[total, field] if cross else field,
        compiler_params=params(),
        cost_estimate=cost(COST[name]),
        name=name,
    )(*flags, block, *operands)


PANEL = 32
GROUP = 8


def lanes(value, width):
    return jnp.concatenate([value] * (width // value.shape[1]), axis=1)


def sublanes(value, height):
    return jnp.concatenate([value] * (height // value.shape[0]), axis=0)


def split3(value):
    high = value.astype(jnp.bfloat16)
    rest = value - high.astype(jnp.float32)
    middle = rest.astype(jnp.bfloat16)
    return high, middle, (rest - middle.astype(jnp.float32)).astype(jnp.bfloat16)


def eliminate(panel, start, at):
    height, size = panel.shape
    first = start + at
    sub = lax.broadcasted_iota(jnp.int32, (height, size), 0)
    lane = lax.broadcasted_iota(jnp.int32, (height, size), 1)
    sub1 = lax.broadcasted_iota(jnp.int32, (height, 128), 0)
    lane8 = lax.broadcasted_iota(jnp.int32, (8, size), 1)
    span = range(GROUP)
    columns = [jnp.broadcast_to(panel[:, first + i : first + i + 1], (height, 128)) for i in span]
    rows = [jnp.broadcast_to(panel[at + i : at + i + 1, :], (8, size)) for i in span]
    entry = {
        (i, k): jnp.broadcast_to(columns[k][at + i : at + i + 1, :], (8, 128))
        for i in span
        for k in range(i, GROUP)
    }
    inverse = []
    for i in span:
        inverse.append(1.0 / entry[i, i])
        rows[i] = jnp.where(lane8 == first + i, 1.0, rows[i])
        for k in range(i + 1, GROUP):
            factor = entry[i, k] * inverse[i]
            rows[k] = jnp.where(lane8 == first + i, 0.0, rows[k]) - lanes(factor, size) * rows[i]
            columns[k] = columns[k] - sublanes(factor, height) * columns[i]
            for j in range(i + 1, k + 1):
                entry[j, k] = entry[j, k] - factor * entry[i, j]
    rows = [
        jnp.where((lane8 > first + i) & (lane8 < first + GROUP), 0.0, rows[i]) for i in span
    ]
    done = at + GROUP
    result = jnp.where((lane >= first) & (lane < first + GROUP) & (sub >= done), 0.0, panel)
    for i in span:
        factor = jnp.where(sub1 >= done, columns[i] * sublanes(inverse[i], height), 0.0)
        result = result - lanes(factor, size) * sublanes(rows[i], height)
    for i in span:
        result = jnp.where(sub == at + i, sublanes(rows[i], height), result)
    return result, [entry[i, i] for i in span]


def rotation_panels(begin, stop, out_ref, work_ref):
    size = work_ref.shape[0]
    sub = lax.broadcasted_iota(jnp.int32, (PANEL, size), 0)
    lane = lax.broadcasted_iota(jnp.int32, (PANEL, size), 1)
    sub1 = lax.broadcasted_iota(jnp.int32, (PANEL, 128), 0)
    for start in range(begin, stop, PANEL):
        end = start + PANEL
        panel = work_ref[start:end, :]
        norm = jnp.zeros((PANEL, 128), jnp.float32)
        for at in range(0, PANEL, GROUP):
            panel, pivots = eliminate(panel, start, at)
            for i, pivot in enumerate(pivots):
                norm = jnp.where(sub1 == at + i, sublanes(lax.rsqrt(pivot), PANEL), norm)
        panel = panel * lanes(norm, size)
        panel = jnp.where((lane > start + sub) & (lane < end), 0.0, panel)
        out_ref[start:end, :] = jnp.where(lane < end, panel, 0.0)
        if end < size:
            high, middle, low = split3(panel)
            right = jnp.concatenate([high, middle, low, high, middle, high], axis=0)
            left = jnp.concatenate(
                [part[:, end:] for part in (high, high, high, middle, middle, low)], axis=0
            )
            update = lax.dot_general(
                left, right, (((0,), (0,)), ((), ())), preferred_element_type=jnp.float32
            )
            rest = work_ref[end:, :]
            place = lax.broadcasted_iota(jnp.int32, rest.shape, 1)
            work_ref[end:, :] = jnp.where((place >= start) & (place < end), 0.0, rest) - update


def rotation_first_kernel(scale, gram_ref, out_ref, work_ref):
    size = work_ref.shape[0]
    half = size // 2
    first, last = unpack(gram_ref[:half, :half] * scale, gram_ref[half : half + 1, :half] * scale)
    work_ref[:half, :half] = first
    work_ref[half:, half:] = last
    work_ref[:half, half:] = gram_ref[:half, half:] * scale
    work_ref[half:, :half] = jnp.zeros((half, half), jnp.float32)
    rotation_panels(0, half, out_ref, work_ref)


def rotation_last_kernel(before_ref, state_ref, out_ref, work_ref):
    size = work_ref.shape[0]
    half = size // 2
    out_ref[:half, :] = before_ref[...]
    work_ref[half:, :] = state_ref[half:, :]
    rotation_panels(half, size, out_ref, work_ref)


def rotation_first(packed, cell_count):
    size = packed.shape[1]
    return pl.pallas_call(
        lambda *refs: rotation_first_kernel(1.0 / cell_count, *refs),
        in_specs=[VMEM],
        out_specs=[VMEM, VMEM],
        out_shape=[
            jax.ShapeDtypeStruct((size // 2, size), jnp.float32),
            jax.ShapeDtypeStruct((size, size), jnp.float32),
        ],
        compiler_params=params(),
        cost_estimate=cost(1),
        name="rotation_first",
    )(packed)


def rotation_last(before, state):
    size = state.shape[0]
    return pl.pallas_call(
        rotation_last_kernel,
        in_specs=[VMEM, VMEM],
        out_specs=VMEM,
        out_shape=jax.ShapeDtypeStruct((size, size), jnp.float32),
        scratch_shapes=[pltpu.VMEM((size, size), jnp.float32)],
        compiler_params=params(),
        cost_estimate=cost(1),
        name="rotation_last",
    )(before, state)


def modes_kernel(first, r_ref, low_ref, mid_ref, top_ref, *refs):
    out_ref = refs[-1]
    high, low = split(r_ref[...])
    v = pl.program_id(0)
    width = mid_ref.shape[4] // 2
    places = [(low_ref, first + v, 0)]
    places += [(mid_ref, v, p) for p in range(mid_ref.shape[2])]
    places += [(top_ref, first + v, 0)]
    rows = []
    for ref, at, p in places:
        large, small = ref[0, at, p], ref[1, at, p]
        value = matmul(high, large) + matmul(high, small) + matmul(low, large)
        value = value.astype(out_ref.dtype)
        rows += [value[:, :width], value[:, width:]]
    out_ref[:, 0] = jnp.swapaxes(jnp.stack(rows, axis=0), 0, 1)


def modes_of(rotation, low, mid, top, first, before):
    variables, (_, span, pairs, size, width) = low.shape[1], mid.shape
    rows, width = 2 * pairs + 4, width // 2
    earlier = [] if before is None else [before]
    return pl.pallas_call(
        lambda *refs: modes_kernel(first, *refs),
        grid=(span,),
        in_specs=[pl.BlockSpec((size, size), lambda v: (0, 0))]
        + [VMEM] * 3
        + [pl.BlockSpec(memory_space=pl.ANY)] * len(earlier),
        out_specs=pl.BlockSpec((size, 1, rows, width), lambda v: (0, first + v, 0, 0)),
        out_shape=jax.ShapeDtypeStruct((size, variables, rows, width), jnp.bfloat16),
        input_output_aliases={4: 0} if earlier else {},
        compiler_params=params(),
        cost_estimate=cost(1 if before is None else 10 * size * size * rows * span * width),
        name="modes",
    )(rotation, low, mid, top, *earlier)


class Sum:
    def __init__(self, value, axis):
        self.axis, self.count = axis, lax.axis_size(axis)
        self.butterfly = self.count >= 2 and not self.count & (self.count - 1)
        if not self.butterfly:
            self.own = value
            return
        half = value.shape[0] // 2
        self.odd = lax.axis_index(axis) % 2 == 1
        first, second = value[:half], value[half:]
        self.own = jnp.where(self.odd, second, first) + self.swap(
            jnp.where(self.odd, first, second), 1
        )

    def swap(self, part, step):
        return lax.ppermute(part, self.axis, [(i, i ^ step) for i in range(self.count)])

    def steps(self):
        return [1 << k for k in range(1, self.count.bit_length() - 1)] if self.butterfly else []

    def add(self, step):
        self.own = self.own + self.swap(self.own, step)

    def result(self):
        if not self.butterfly:
            return lax.psum(self.own, self.axis)
        other = self.swap(self.own, 1)
        low, high = jnp.where(self.odd, other, self.own), jnp.where(self.odd, self.own, other)
        return jnp.concatenate([low, high], axis=0)


def shifted(value, axis, step):
    count = lax.axis_size(axis)
    pairs = [(i, i + step) for i in range(count) if 0 <= i + step < count]
    return lax.ppermute(value, axis, pairs)


def swapped(block, weights, diffusivity, axis):
    devices = lax.axis_size(axis)
    _, rows, variables, count, width = block.shape
    odd = lax.axis_index(axis) % 2 == 1
    factor = weights[None, rows - 2 :] * (diffusivity[:, rows - 2 :] * (1.0 / 12.0))
    top = lax.reduce_precision(factor, 8, 7)
    middle = lax.reduce_precision(factor - top, 8, 7)
    parts = jnp.stack([top, middle, factor - top - middle], axis=2).astype(block.dtype)
    parts = parts.transpose(1, 0, 2, 3)
    parts = jnp.pad(parts, ((0, 0), (0, 0), (0, count - 3), (0, 0)))[None]
    sent = [
        jnp.concatenate([lax.dynamic_slice_in_dim(block, start, 2, axis=1), parts], axis=0)
        for start in (jnp.where(odd, 0, rows - 2), jnp.where(odd, rows - 2, 0))
    ]
    *sent, block = lax.optimization_barrier((*sent, block))
    received = []
    for first, part in enumerate(sent):
        pairs = [(i, i + 1) for i in range(first, devices - 1, 2)]
        received.append(lax.ppermute(part, axis, pairs + [(b, a) for a, b in pairs]))
    return block, received


def on_device(snapshots, cell_weights, diffusivity):
    highest = lax.Precision.HIGHEST
    together = lax.optimization_barrier
    owners = lax.axis_size("gx")
    block = lax.all_to_all(relayout(snapshots, owners), "gx", 0, 0, tiled=True)
    if snapshots.shape[0] % 16:
        count, rows, variables, each, width = block.shape
        block = block.transpose(1, 2, 0, 3, 4).reshape(1, rows, variables, count * each, width)
    _, rows, variables, count, width = block.shape
    size, cell_count = block.shape[0] * count, rows * variables * width * owners
    band = band_matrix(width)
    half = variables // 2
    spans = [span for span in (range(half), range(half, variables)) if len(span)]

    odd = (lax.axis_index("gx") % 2).astype(jnp.int32).reshape(1)
    block, (near, far) = swapped(block, cell_weights, diffusivity, "gx")
    block, near = together((block, near))
    packed, kept = gram_of(block, cell_weights)
    cross = jnp.zeros((size, size), jnp.float32)
    mids = []

    def inner(span, kept, cross):
        cross, mid = stencil_call(
            functools.partial(inner_kernel, span), "inner", kept, len(span), rows // 2 - 2, True,
            cell_weights, diffusivity, band, cross,
        )
        mids.append(mid)
        return cross

    gram = Sum(packed, "gx")
    steps = gram.steps()
    kept, gram.own = together((kept, gram.own))
    for span in spans:
        cross = inner(span, kept, cross)
    cross, bottom = stencil_call(
        lower_kernel, "lower", kept, variables, 1, True,
        near, far, cell_weights, diffusivity, band, cross, odd=odd,
    )
    if steps:
        gram.add(steps.pop(0))
    cross, gram.own = together((cross, gram.own))
    cross = Sum(cross, "gx")
    while steps:
        gram.add(steps.pop(0))
    steps = cross.steps()
    if steps:
        cross.add(steps.pop(0))
    top = stencil_call(
        upper_kernel, "upper", kept, variables, 1, False, near, far, diffusivity, band, odd=odd
    )
    gram.own, cross.own, top = together((gram.own, cross.own, top))
    state = rotation_first(gram.result(), cell_count)
    if steps:
        cross.add(steps.pop(0))
    state, cross.own = together((state, cross.own))
    rotation = rotation_last(*state)
    while steps:
        cross.add(steps.pop(0))
    modes = None
    for span, mid in zip(spans, mids):
        if modes is not None:
            modes, cross.own = together((modes, cross.own))
        modes = modes_of(rotation, bottom, mid, top, span[0], modes)
    cross_total = cross.result() * (1.0 / cell_count)
    reduced = jnp.dot(
        jnp.dot(rotation, cross_total.T, precision=highest), rotation.T, precision=highest
    )
    return (modes, reduced)


def solution(mesh):
    in_specs = (
        P("gx", None, "groups", None),
        P(("groups", "gx"), None),
        P(None, ("groups", "gx"), None),
    )
    out_specs = (P(None, None, ("groups", "gx"), None), P("groups", None))
    return jax.shard_map(
        on_device, mesh=mesh, in_specs=in_specs, out_specs=out_specs, check_vma=False
    )
```

```python
import functools

import jax
import jax.numpy as jnp
from jax import lax
from jax.experimental import pallas as pl
from jax.experimental.pallas import tpu as pltpu
from jax.sharding import PartitionSpec as P

VMEM_LIMIT = 24 * 1024 * 1024
NT = (((1,), (1,)), ((), ()))


def cost(flops):
    return pl.CostEstimate(flops=int(flops), bytes_accessed=1, transcendentals=0)


VMEM = pl.BlockSpec(memory_space=pltpu.VMEM)


def params():
    return pltpu.CompilerParams(vmem_limit_bytes=VMEM_LIMIT)


def split(value):
    high = value.astype(jnp.bfloat16)
    low = (value - high.astype(jnp.float32)).astype(jnp.bfloat16)
    return high, low


def matmul(a, b):
    return jnp.dot(a, b, preferred_element_type=jnp.float32)


def matmul_nt(a, b):
    return lax.dot_general(a, b, NT, preferred_element_type=jnp.float32)


def relayout_kernel(in_ref, out_ref):
    owners, rows, variables = out_ref.shape[:3]
    for owner in range(owners):
        for v in range(variables):
            block = in_ref[:, v, owner * rows : (owner + 1) * rows]
            out_ref[owner, :, v] = jnp.swapaxes(block, 0, 1)


def relayout(snapshots, owners):
    count, variables, cells, width = snapshots.shape
    rows = cells // owners
    if count % 16 or rows % 16:
        block = snapshots.reshape(count, variables, owners, rows, width)
        return block.transpose(2, 3, 1, 0, 4)
    each = owners // 2 if owners % 2 == 0 else 1
    return pl.pallas_call(
        relayout_kernel,
        grid=(owners // each,),
        in_specs=[pl.BlockSpec((count, variables, each * rows, width), lambda i: (0, 0, i, 0))],
        out_specs=pl.BlockSpec(
            (each, rows, variables, count, width), lambda i: (i, 0, 0, 0, 0)
        ),
        out_shape=jax.ShapeDtypeStruct((owners, rows, variables, count, width), snapshots.dtype),
        compiler_params=pltpu.CompilerParams(vmem_limit_bytes=60 * 1024 * 1024),
        name="relayout",
    )(snapshots)


def row_of(ref, x, v):
    value = ref[:, x, v]
    return value.reshape(value.shape[0] * value.shape[1], value.shape[2])


def pack(gram):
    half = gram.shape[0] // 2
    sub = lax.broadcasted_iota(jnp.int32, (half, half), 0)
    lane = lax.broadcasted_iota(jnp.int32, (half, half), 1)
    first, last = gram[:half, :half], gram[half:, half:]
    diagonal = jnp.sum(jnp.where(lane == sub, first, 0.0), axis=0, keepdims=True)
    mixed = jnp.where(lane > sub, first, last)
    top = jnp.concatenate([mixed, gram[:half, half:]], axis=1)
    return top, jnp.broadcast_to(jnp.concatenate([diagonal, diagonal], axis=1), (16, 2 * half))


def unpack(mixed, diagonal):
    half = mixed.shape[0]
    sub = lax.broadcasted_iota(jnp.int32, (half, half), 0)
    lane = lax.broadcasted_iota(jnp.int32, (half, half), 1)
    upper = jnp.where(lane > sub, mixed, 0.0)
    lower = jnp.where(lane < sub, mixed, 0.0)
    first = jnp.where(lane == sub, diagonal, upper + upper.T)
    last = jnp.where(lane == sub, mixed, lower + lower.T)
    return first, last


def gram_kernel(x_ref, w_ref, out_ref, keep_ref, first_ref, total_ref):
    rows, each = x_ref.shape[1:3]
    size = total_ref.shape[0]

    @pl.when(pl.program_id(0) == 0)
    def _():
        total_ref[...] = jnp.zeros_like(total_ref)

    total = None
    for v in range(each):
        for first in range(0, rows, 4):
            group = range(first, first + 4)
            plain = [row_of(x_ref, x, v) for x in group]
            at = pl.program_id(0) * each + v
            for x in group:
                keep_ref[at, x] = plain[x - first]
                if x < 2:
                    first_ref[x, at] = plain[x - first]
            plain = jnp.concatenate(plain, axis=1)
            weight = jnp.concatenate([w_ref[x : x + 1, :] for x in group], axis=1)
            high, low = split(plain.astype(jnp.float32) * weight)
            term = matmul_nt(high, plain) + matmul_nt(low, plain)
            total = term if total is None else total + term
    total_ref[...] += total

    @pl.when(pl.program_id(0) == pl.num_programs(0) - 1)
    def _():
        top, diagonal = pack(total_ref[...])
        out_ref[: size // 2, :] = top
        out_ref[size // 2 :, :] = diagonal


def gram_of(block, weights):
    owners, rows, variables, count, width = block.shape
    size = owners * count
    each = 2 if variables % 2 == 0 else 1
    return pl.pallas_call(
        gram_kernel,
        grid=(variables // each,),
        in_specs=[
            pl.BlockSpec((owners, rows, each, count, width), lambda v: (0, 0, v, 0, 0)),
            pl.BlockSpec((rows, width), lambda v: (0, 0)),
        ],
        out_specs=[pl.BlockSpec((size // 2 + 16, size), lambda v: (0, 0)), VMEM, VMEM],
        out_shape=[
            jax.ShapeDtypeStruct((size // 2 + 16, size), jnp.float32),
            jax.ShapeDtypeStruct((variables, rows, size, width), block.dtype),
            jax.ShapeDtypeStruct((2, variables, size, width), block.dtype),
        ],
        scratch_shapes=[pltpu.VMEM((size, size), jnp.float32)],
        compiler_params=params(),
        cost_estimate=cost(2e9),
        name="gram",
    )(block, weights)


def along_x(lower, upper, centre):
    near = [part for part in (lower[1], upper[0]) if part is not None]
    far = [part for part in (lower[0], upper[1]) if part is not None]
    value = 16.0 * sum(near[1:], near[0]) if near else jnp.zeros_like(centre)
    return value - sum(far[1:], far[0]) if far else value


def two(ref, x):
    return jnp.concatenate([ref[x : x + 1, :], ref[x + 1 : x + 2, :]], axis=1)


def stencil(value, x, pair, d_ref, band_ref):
    sides = [
        along_x((value.get(k - 2), value.get(k - 1)), (value.get(k + 1), value.get(k + 2)), value[k])
        for k in (x, x + 1)
    ]
    both = matmul(pair, band_ref[...]) + jnp.concatenate(sides, axis=1)
    return both * (two(d_ref, x) * (1.0 / 12.0))


def products(left, right):
    term = matmul_nt(jnp.concatenate(split(left), axis=0), right)
    half = term.shape[0] // 2
    return term[:half] + term[half:]


def store(f_ref, v, p, field):
    f_ref[0, v, p], f_ref[1, v, p] = split(field)


def inner_kernel(span, x_ref, w_ref, d_ref, band_ref, before_ref, cross_ref, f_ref):
    rows = x_ref.shape[1]
    cross_ref[...] = before_ref[...]
    for place, v in enumerate(span):
        plain = [x_ref[v, x] for x in range(rows)]
        value = {x: part.astype(jnp.float32) for x, part in enumerate(plain)}
        total = None
        for x in range(2, rows, 2):
            pair = jnp.concatenate(plain[x : x + 2], axis=1)
            field = stencil(value, x, pair, d_ref.at[v], band_ref)
            if x < rows - 2:
                store(f_ref, place, x // 2 - 1, field)
            term = products(field * two(w_ref, x), pair)
            total = term if total is None else total + term
        cross_ref[...] += total


def lower_kernel(odd_ref, x_ref, near_ref, far_ref, w_ref, d_ref, band_ref, before_ref, cross_ref, f_ref):
    variables, owners = x_ref.shape[0], near_ref.shape[0] - 1
    odd = odd_ref[0] == 1
    cross_ref[...] = before_ref[...]
    for v in range(variables):
        plain = {x: x_ref[v, x] for x in range(4)}
        for x in range(2):
            near, far = (row_of(ref.at[:owners], x, v) for ref in (near_ref, far_ref))
            plain[x - 2] = jnp.where(odd, near, far)
        value = {x: part.astype(jnp.float32) for x, part in plain.items()}
        pair = jnp.concatenate([plain[0], plain[1]], axis=1)
        field = stencil(value, 0, pair, d_ref.at[v], band_ref)
        store(f_ref, v, 0, field)
        total = products(field * two(w_ref, 0), pair)
        factor = []
        for x in range(2):
            near, far = (ref[owners, x, v].astype(jnp.float32) for ref in (near_ref, far_ref))
            parts = jnp.where(odd, near, far)
            factor.append(parts[0:1] + parts[1:2] + parts[2:3])
        joined = jnp.concatenate(
            [-value[0] * factor[0], (16.0 * value[0] - value[1]) * factor[1]], axis=1
        )
        total = total + products(joined, jnp.concatenate([plain[-2], plain[-1]], axis=1))
        cross_ref[...] += total


def upper_kernel(odd_ref, x_ref, near_ref, far_ref, d_ref, band_ref, f_ref):
    variables, rows = x_ref.shape[:2]
    owners = near_ref.shape[0] - 1
    odd = odd_ref[0] == 1
    for v in range(variables):
        plain = {x: x_ref[v, x] for x in range(rows - 4, rows)}
        for x in range(2):
            near = row_of(near_ref.at[:owners], x, v)
            plain[rows + x] = jnp.where(odd, far_ref[x, v], near)
        value = {x: part.astype(jnp.float32) for x, part in plain.items()}
        pair = jnp.concatenate([plain[rows - 2], plain[rows - 1]], axis=1)
        store(f_ref, v, 0, stencil(value, rows - 2, pair, d_ref.at[v], band_ref))


def band_matrix(width):
    shape = (2, width, 2, width)
    i, y, j, z = (lax.broadcasted_iota(jnp.int32, shape, axis) for axis in range(4))
    distance = jnp.abs(y - z)
    line = jnp.where(
        distance == 0, -60.0, jnp.where(distance == 1, 16.0, jnp.where(distance == 2, -1.0, 0.0))
    )
    return jnp.where(i == j, line, 0.0).reshape(2 * width, 2 * width).astype(jnp.bfloat16)


COST = {"inner": 1, "lower": 1, "upper": 1}


def stencil_call(kernel, name, block, span, pairs, cross, *operands, odd=None):
    _, _, size, width = block.shape
    field = jax.ShapeDtypeStruct((2, span, pairs, size, 2 * width), jnp.bfloat16)
    total = jax.ShapeDtypeStruct((size, size), jnp.float32)
    flags = [] if odd is None else [odd]
    return pl.pallas_call(
        kernel,
        in_specs=[pl.BlockSpec(memory_space=pltpu.SMEM)] * len(flags) + [VMEM] * (1 + len(operands)),
        out_specs=[VMEM, VMEM] if cross else VMEM,
        out_shape=[total, field] if cross else field,
        compiler_params=params(),
        cost_estimate=cost(COST[name]),
        name=name,
    )(*flags, block, *operands)


PANEL = 32
GROUP = 8


def lanes(value, width):
    return jnp.concatenate([value] * (width // value.shape[1]), axis=1)


def sublanes(value, height):
    return jnp.concatenate([value] * (height // value.shape[0]), axis=0)


def split3(value):
    high = value.astype(jnp.bfloat16)
    rest = value - high.astype(jnp.float32)
    middle = rest.astype(jnp.bfloat16)
    return high, middle, (rest - middle.astype(jnp.float32)).astype(jnp.bfloat16)


def eliminate(panel, start, at):
    height, size = panel.shape
    first = start + at
    sub = lax.broadcasted_iota(jnp.int32, (height, size), 0)
    lane = lax.broadcasted_iota(jnp.int32, (height, size), 1)
    sub1 = lax.broadcasted_iota(jnp.int32, (height, 128), 0)
    lane8 = lax.broadcasted_iota(jnp.int32, (8, size), 1)
    span = range(GROUP)
    columns = [jnp.broadcast_to(panel[:, first + i : first + i + 1], (height, 128)) for i in span]
    rows = [jnp.broadcast_to(panel[at + i : at + i + 1, :], (8, size)) for i in span]
    entry = {
        (i, k): jnp.broadcast_to(columns[k][at + i : at + i + 1, :], (8, 128))
        for i in span
        for k in range(i, GROUP)
    }
    inverse = []
    for i in span:
        inverse.append(1.0 / entry[i, i])
        rows[i] = jnp.where(lane8 == first + i, 1.0, rows[i])
        for k in range(i + 1, GROUP):
            factor = entry[i, k] * inverse[i]
            rows[k] = jnp.where(lane8 == first + i, 0.0, rows[k]) - lanes(factor, size) * rows[i]
            columns[k] = columns[k] - sublanes(factor, height) * columns[i]
            for j in range(i + 1, k + 1):
                entry[j, k] = entry[j, k] - factor * entry[i, j]
    rows = [
        jnp.where((lane8 > first + i) & (lane8 < first + GROUP), 0.0, rows[i]) for i in span
    ]
    done = at + GROUP
    result = jnp.where((lane >= first) & (lane < first + GROUP) & (sub >= done), 0.0, panel)
    for i in span:
        factor = jnp.where(sub1 >= done, columns[i] * sublanes(inverse[i], height), 0.0)
        result = result - lanes(factor, size) * sublanes(rows[i], height)
    for i in span:
        result = jnp.where(sub == at + i, sublanes(rows[i], height), result)
    return result, [entry[i, i] for i in span]


def rotation_panels(begin, stop, out_ref, work_ref):
    size = work_ref.shape[0]
    sub = lax.broadcasted_iota(jnp.int32, (PANEL, size), 0)
    lane = lax.broadcasted_iota(jnp.int32, (PANEL, size), 1)
    sub1 = lax.broadcasted_iota(jnp.int32, (PANEL, 128), 0)
    for start in range(begin, stop, PANEL):
        end = start + PANEL
        panel = work_ref[start:end, :]
        norm = jnp.zeros((PANEL, 128), jnp.float32)
        for at in range(0, PANEL, GROUP):
            panel, pivots = eliminate(panel, start, at)
            for i, pivot in enumerate(pivots):
                norm = jnp.where(sub1 == at + i, sublanes(lax.rsqrt(pivot), PANEL), norm)
        panel = panel * lanes(norm, size)
        panel = jnp.where((lane > start + sub) & (lane < end), 0.0, panel)
        out_ref[start:end, :] = jnp.where(lane < end, panel, 0.0)
        if end < size:
            high, middle, low = split3(panel)
            right = jnp.concatenate([high, middle, low, high, middle, high], axis=0)
            left = jnp.concatenate(
                [part[:, end:] for part in (high, high, high, middle, middle, low)], axis=0
            )
            update = lax.dot_general(
                left, right, (((0,), (0,)), ((), ())), preferred_element_type=jnp.float32
            )
            rest = work_ref[end:, :]
            place = lax.broadcasted_iota(jnp.int32, rest.shape, 1)
            work_ref[end:, :] = jnp.where((place >= start) & (place < end), 0.0, rest) - update


def rotation_first_kernel(scale, gram_ref, out_ref, work_ref):
    size = work_ref.shape[0]
    half = size // 2
    first, last = unpack(gram_ref[:half, :half] * scale, gram_ref[half : half + 1, :half] * scale)
    work_ref[:half, :half] = first
    work_ref[half:, half:] = last
    work_ref[:half, half:] = gram_ref[:half, half:] * scale
    work_ref[half:, :half] = jnp.zeros((half, half), jnp.float32)
    rotation_panels(0, half, out_ref, work_ref)


def rotation_last_kernel(before_ref, state_ref, out_ref, work_ref):
    size = work_ref.shape[0]
    half = size // 2
    out_ref[:half, :] = before_ref[...]
    work_ref[half:, :] = state_ref[half:, :]
    rotation_panels(half, size, out_ref, work_ref)


def rotation_first(packed, cell_count):
    size = packed.shape[1]
    return pl.pallas_call(
        lambda *refs: rotation_first_kernel(1.0 / cell_count, *refs),
        in_specs=[VMEM],
        out_specs=[VMEM, VMEM],
        out_shape=[
            jax.ShapeDtypeStruct((size // 2, size), jnp.float32),
            jax.ShapeDtypeStruct((size, size), jnp.float32),
        ],
        compiler_params=params(),
        cost_estimate=cost(1),
        name="rotation_first",
    )(packed)


def rotation_last(before, state):
    size = state.shape[0]
    return pl.pallas_call(
        rotation_last_kernel,
        in_specs=[VMEM, VMEM],
        out_specs=VMEM,
        out_shape=jax.ShapeDtypeStruct((size, size), jnp.float32),
        scratch_shapes=[pltpu.VMEM((size, size), jnp.float32)],
        compiler_params=params(),
        cost_estimate=cost(1),
        name="rotation_last",
    )(before, state)


def modes_kernel(first, r_ref, low_ref, mid_ref, top_ref, *refs):
    out_ref = refs[-1]
    high, low = split(r_ref[...])
    v = pl.program_id(0)
    width = mid_ref.shape[4] // 2
    places = [(low_ref, first + v, 0)]
    places += [(mid_ref, v, p) for p in range(mid_ref.shape[2])]
    places += [(top_ref, first + v, 0)]
    rows = []
    for ref, at, p in places:
        large, small = ref[0, at, p], ref[1, at, p]
        value = matmul(high, large) + matmul(high, small) + matmul(low, large)
        value = value.astype(out_ref.dtype)
        rows += [value[:, :width], value[:, width:]]
    out_ref[:, 0] = jnp.swapaxes(jnp.stack(rows, axis=0), 0, 1)


def modes_of(rotation, low, mid, top, first, before):
    variables, (_, span, pairs, size, width) = low.shape[1], mid.shape
    rows, width = 2 * pairs + 4, width // 2
    earlier = [] if before is None else [before]
    return pl.pallas_call(
        lambda *refs: modes_kernel(first, *refs),
        grid=(span,),
        in_specs=[pl.BlockSpec((size, size), lambda v: (0, 0))]
        + [VMEM] * 3
        + [pl.BlockSpec(memory_space=pl.ANY)] * len(earlier),
        out_specs=pl.BlockSpec((size, 1, rows, width), lambda v: (0, first + v, 0, 0)),
        out_shape=jax.ShapeDtypeStruct((size, variables, rows, width), jnp.bfloat16),
        input_output_aliases={4: 0} if earlier else {},
        compiler_params=params(),
        cost_estimate=cost(1 if before is None else 10 * size * size * rows * span * width),
        name="modes",
    )(rotation, low, mid, top, *earlier)


class Sum:
    def __init__(self, value, axis):
        self.axis, self.count = axis, lax.axis_size(axis)
        self.butterfly = self.count >= 2 and not self.count & (self.count - 1)
        if not self.butterfly:
            self.own = value
            return
        half = value.shape[0] // 2
        self.odd = lax.axis_index(axis) % 2 == 1
        first, second = value[:half], value[half:]
        self.own = jnp.where(self.odd, second, first) + self.swap(
            jnp.where(self.odd, first, second), 1
        )

    def swap(self, part, step):
        return lax.ppermute(part, self.axis, [(i, i ^ step) for i in range(self.count)])

    def steps(self):
        return [1 << k for k in range(1, self.count.bit_length() - 1)] if self.butterfly else []

    def add(self, step):
        self.own = self.own + self.swap(self.own, step)

    def result(self):
        if not self.butterfly:
            return lax.psum(self.own, self.axis)
        other = self.swap(self.own, 1)
        low, high = jnp.where(self.odd, other, self.own), jnp.where(self.odd, self.own, other)
        return jnp.concatenate([low, high], axis=0)


def shifted(value, axis, step):
    count = lax.axis_size(axis)
    pairs = [(i, i + step) for i in range(count) if 0 <= i + step < count]
    return lax.ppermute(value, axis, pairs)


def hop(value, axis, first, step):
    devices = lax.axis_size(axis)
    return lax.ppermute(
        value, axis, [(i, i + step) for i in range(first, devices, 2) if 0 <= i + step < devices]
    )


def lower_rows(block, weights, diffusivity, axis):
    devices = lax.axis_size(axis)
    _, rows, variables, count, width = block.shape
    odd = lax.axis_index(axis) % 2 == 1
    factor = weights[None, rows - 2 :] * (diffusivity[:, rows - 2 :] * (1.0 / 12.0))
    top = lax.reduce_precision(factor, 8, 7)
    middle = lax.reduce_precision(factor - top, 8, 7)
    parts = jnp.stack([top, middle, factor - top - middle], axis=2).astype(block.dtype)
    parts = parts.transpose(1, 0, 2, 3)
    parts = jnp.pad(parts, ((0, 0), (0, 0), (0, count - 3), (0, 0)))[None]
    near, far = [
        jnp.concatenate([lax.dynamic_slice_in_dim(block, start, 2, axis=1), parts], axis=0)
        for start in (jnp.where(odd, 0, rows - 2), rows - 2)
    ]
    near, far, block = lax.optimization_barrier((near, far, block))
    pairs = [(i, i + 1) for i in range(0, devices - 1, 2)]
    near = lax.ppermute(near, axis, pairs + [(b, a) for a, b in pairs])
    return block, near, hop(far, axis, 1, 1)


def on_device(snapshots, cell_weights, diffusivity):
    highest = lax.Precision.HIGHEST
    together = lax.optimization_barrier
    owners = lax.axis_size("gx")
    block = lax.all_to_all(relayout(snapshots, owners), "gx", 0, 0, tiled=True)
    if snapshots.shape[0] % 16:
        count, rows, variables, each, width = block.shape
        block = block.transpose(1, 2, 0, 3, 4).reshape(1, rows, variables, count * each, width)
    _, rows, variables, count, width = block.shape
    size, cell_count = block.shape[0] * count, rows * variables * width * owners
    band = band_matrix(width)
    half = variables - variables // 4
    spans = [span for span in (range(half), range(half, variables)) if len(span)]

    odd = (lax.axis_index("gx") % 2).astype(jnp.int32).reshape(1)
    block, near, far = lower_rows(block, cell_weights, diffusivity, "gx")
    block, near = together((block, near))
    packed, kept, first_rows = gram_of(block, cell_weights)
    cross = jnp.zeros((size, size), jnp.float32)
    mids = []

    def inner(span, kept, cross):
        cross, mid = stencil_call(
            functools.partial(inner_kernel, span), "inner", kept, len(span), rows // 2 - 2, True,
            cell_weights, diffusivity, band, cross,
        )
        mids.append(mid)
        return cross

    gram = Sum(packed, "gx")
    steps = gram.steps()
    kept, first_rows, gram.own = together((kept, first_rows, gram.own))
    above = hop(first_rows, "gx", 0, -1)
    for span in spans:
        if mids:
            kept, cross, gram.own = together((kept, cross, gram.own))
        cross = inner(span, kept, cross)
        if steps:
            gram.add(steps.pop(0))
    kept, cross, gram.own = together((kept, cross, gram.own))
    cross, bottom = stencil_call(
        lower_kernel, "lower", kept, variables, 1, True,
        near, far, cell_weights, diffusivity, band, cross, odd=odd,
    )
    cross = Sum(cross, "gx")
    while steps:
        gram.add(steps.pop(0))
    steps = cross.steps()
    if steps:
        cross.add(steps.pop(0))
    top = stencil_call(
        upper_kernel, "upper", kept, variables, 1, False, near, above, diffusivity, band, odd=odd
    )
    gram.own, top = together((gram.own, top))
    packed, cross.own = together((gram.result(), cross.own))
    state = rotation_first(packed, cell_count)
    if steps:
        cross.add(steps.pop(0))
    state, cross.own = together((state, cross.own))
    rotation = rotation_last(*state)
    while steps:
        cross.add(steps.pop(0))
    modes = None
    for span, mid in zip(spans, mids):
        if modes is not None:
            modes, cross.own = together((modes, cross.own))
        modes = modes_of(rotation, bottom, mid, top, span[0], modes)
    cross_total = cross.result() * (1.0 / cell_count)
    reduced = jnp.dot(
        jnp.dot(rotation, cross_total.T, precision=highest), rotation.T, precision=highest
    )
    return (modes, reduced)


def solution(mesh):
    in_specs = (
        P("gx", None, "groups", None),
        P(("groups", "gx"), None),
        P(None, ("groups", "gx"), None),
    )
    out_specs = (P(None, None, ("groups", "gx"), None), P("groups", None))
    return jax.shard_map(
        on_device, mesh=mesh, in_specs=in_specs, out_specs=out_specs, check_vma=False
    )
```

```python
import functools
import math

import jax
import jax.numpy as jnp
from jax import lax
from jax.experimental import pallas as pl
from jax.experimental.pallas import tpu as pltpu
from jax.sharding import PartitionSpec as P

VMEM_LIMIT = 24 * 1024 * 1024
NT = (((1,), (1,)), ((), ()))


def cost(flops):
    return pl.CostEstimate(flops=int(flops), bytes_accessed=1, transcendentals=0)


VMEM = pl.BlockSpec(memory_space=pltpu.VMEM)


def params():
    return pltpu.CompilerParams(vmem_limit_bytes=VMEM_LIMIT)


def split(value):
    high = value.astype(jnp.bfloat16)
    low = (value - high.astype(jnp.float32)).astype(jnp.bfloat16)
    return high, low


def matmul(a, b):
    return jnp.dot(a, b, preferred_element_type=jnp.float32)


def matmul_nt(a, b):
    return lax.dot_general(a, b, NT, preferred_element_type=jnp.float32)


def relayout_kernel(reads, writes, in_ref, out_ref, from_ref, to_ref, read_sems, write_sems):
    owners, rows, variables = to_ref.shape[:3]
    each_read, each_write = owners // reads, owners // writes
    arriving = []
    for i in range(reads):
        span = pl.ds(i * each_read * rows, each_read * rows)
        arriving.append(
            pltpu.make_async_copy(in_ref.at[:, :, span], from_ref.at[:, :, span], read_sems.at[i])
        )
        arriving[i].start()
    leaving = []
    for i in range(writes):
        for owner in range(i * each_write, (i + 1) * each_write):
            if owner % each_read == 0:
                arriving[owner // each_read].wait()
            for v in range(variables):
                block = from_ref[:, v, owner * rows : (owner + 1) * rows]
                to_ref[owner, :, v] = jnp.swapaxes(block, 0, 1)
        span = pl.ds(i * each_write, each_write)
        leaving.append(pltpu.make_async_copy(to_ref.at[span], out_ref.at[span], write_sems.at[i]))
        leaving[i].start()
    for copy in leaving:
        copy.wait()


def relayout(snapshots, owners):
    count, variables, cells, width = snapshots.shape
    rows = cells // owners
    if count % 16 or rows % 16:
        block = snapshots.reshape(count, variables, owners, rows, width)
        return block.transpose(2, 3, 1, 0, 4)
    reads, writes = math.gcd(owners, 4), math.gcd(owners, 8)
    shape = (owners, rows, variables, count, width)
    return pl.pallas_call(
        functools.partial(relayout_kernel, reads, writes),
        in_specs=[pl.BlockSpec(memory_space=pl.ANY)],
        out_specs=pl.BlockSpec(memory_space=pl.ANY),
        out_shape=jax.ShapeDtypeStruct(shape, snapshots.dtype),
        scratch_shapes=[
            pltpu.VMEM(snapshots.shape, snapshots.dtype),
            pltpu.VMEM(shape, snapshots.dtype),
            pltpu.SemaphoreType.DMA((reads,)),
            pltpu.SemaphoreType.DMA((writes,)),
        ],
        compiler_params=pltpu.CompilerParams(vmem_limit_bytes=60 * 1024 * 1024),
        name="relayout",
    )(snapshots)


def row_of(ref, x, v):
    value = ref[:, x, v]
    return value.reshape(value.shape[0] * value.shape[1], value.shape[2])


def pack(gram):
    half = gram.shape[0] // 2
    sub = lax.broadcasted_iota(jnp.int32, (half, half), 0)
    lane = lax.broadcasted_iota(jnp.int32, (half, half), 1)
    first, last = gram[:half, :half], gram[half:, half:]
    diagonal = jnp.sum(jnp.where(lane == sub, first, 0.0), axis=0, keepdims=True)
    mixed = jnp.where(lane > sub, first, last)
    top = jnp.concatenate([mixed, gram[:half, half:]], axis=1)
    return top, jnp.broadcast_to(jnp.concatenate([diagonal, diagonal], axis=1), (16, 2 * half))


def unpack(mixed, diagonal):
    half = mixed.shape[0]
    sub = lax.broadcasted_iota(jnp.int32, (half, half), 0)
    lane = lax.broadcasted_iota(jnp.int32, (half, half), 1)
    upper = jnp.where(lane > sub, mixed, 0.0)
    lower = jnp.where(lane < sub, mixed, 0.0)
    first = jnp.where(lane == sub, diagonal, upper + upper.T)
    last = jnp.where(lane == sub, mixed, lower + lower.T)
    return first, last


def gram_kernel(x_ref, w_ref, out_ref, keep_ref, first_ref, total_ref):
    rows, each = x_ref.shape[1:3]
    size = total_ref.shape[0]

    @pl.when(pl.program_id(0) == 0)
    def _():
        total_ref[...] = jnp.zeros_like(total_ref)

    total = None
    for v in range(each):
        for first in range(0, rows, 4):
            group = range(first, first + 4)
            plain = [row_of(x_ref, x, v) for x in group]
            at = pl.program_id(0) * each + v
            for x in group:
                keep_ref[at, x] = plain[x - first]
                if x < 2:
                    first_ref[x, at] = plain[x - first]
            plain = jnp.concatenate(plain, axis=1)
            weight = jnp.concatenate([w_ref[x : x + 1, :] for x in group], axis=1)
            high, low = split(plain.astype(jnp.float32) * weight)
            term = matmul_nt(high, plain) + matmul_nt(low, plain)
            total = term if total is None else total + term
    total_ref[...] += total

    @pl.when(pl.program_id(0) == pl.num_programs(0) - 1)
    def _():
        top, diagonal = pack(total_ref[...])
        out_ref[: size // 2, :] = top
        out_ref[size // 2 :, :] = diagonal


def gram_of(block, weights):
    owners, rows, variables, count, width = block.shape
    size = owners * count
    each = 2 if variables % 2 == 0 else 1
    return pl.pallas_call(
        gram_kernel,
        grid=(variables // each,),
        in_specs=[
            pl.BlockSpec((owners, rows, each, count, width), lambda v: (0, 0, v, 0, 0)),
            pl.BlockSpec((rows, width), lambda v: (0, 0)),
        ],
        out_specs=[pl.BlockSpec((size // 2 + 16, size), lambda v: (0, 0)), VMEM, VMEM],
        out_shape=[
            jax.ShapeDtypeStruct((size // 2 + 16, size), jnp.float32),
            jax.ShapeDtypeStruct((variables, rows, size, width), block.dtype),
            jax.ShapeDtypeStruct((2, variables, size, width), block.dtype),
        ],
        scratch_shapes=[pltpu.VMEM((size, size), jnp.float32)],
        compiler_params=params(),
        cost_estimate=cost(2e9),
        name="gram",
    )(block, weights)


def along_x(lower, upper, centre):
    near = [part for part in (lower[1], upper[0]) if part is not None]
    far = [part for part in (lower[0], upper[1]) if part is not None]
    value = 16.0 * sum(near[1:], near[0]) if near else jnp.zeros_like(centre)
    return value - sum(far[1:], far[0]) if far else value


def two(ref, x):
    return jnp.concatenate([ref[x : x + 1, :], ref[x + 1 : x + 2, :]], axis=1)


def stencil(value, x, pair, d_ref, band_ref):
    sides = [
        along_x((value.get(k - 2), value.get(k - 1)), (value.get(k + 1), value.get(k + 2)), value[k])
        for k in (x, x + 1)
    ]
    both = matmul(pair, band_ref[...]) + jnp.concatenate(sides, axis=1)
    return both * (two(d_ref, x) * (1.0 / 12.0))


def products(left, right):
    term = matmul_nt(jnp.concatenate(split(left), axis=0), right)
    half = term.shape[0] // 2
    return term[:half] + term[half:]


def store(f_ref, v, p, field):
    f_ref[0, v, p], f_ref[1, v, p] = split(field)


def inner_kernel(span, x_ref, w_ref, d_ref, band_ref, before_ref, cross_ref, f_ref):
    rows = x_ref.shape[1]
    cross_ref[...] = before_ref[...]
    for place, v in enumerate(span):
        plain = [x_ref[v, x] for x in range(rows)]
        value = {x: part.astype(jnp.float32) for x, part in enumerate(plain)}
        total = None
        for x in range(2, rows, 2):
            pair = jnp.concatenate(plain[x : x + 2], axis=1)
            field = stencil(value, x, pair, d_ref.at[v], band_ref)
            if x < rows - 2:
                store(f_ref, place, x // 2 - 1, field)
            term = products(field * two(w_ref, x), pair)
            total = term if total is None else total + term
        cross_ref[...] += total


def lower_kernel(odd_ref, x_ref, near_ref, far_ref, w_ref, d_ref, band_ref, before_ref, cross_ref, f_ref):
    variables, owners = x_ref.shape[0], near_ref.shape[0] - 1
    odd = odd_ref[0] == 1
    cross_ref[...] = before_ref[...]
    for v in range(variables):
        plain = {x: x_ref[v, x] for x in range(4)}
        for x in range(2):
            near, far = (row_of(ref.at[:owners], x, v) for ref in (near_ref, far_ref))
            plain[x - 2] = jnp.where(odd, near, far)
        value = {x: part.astype(jnp.float32) for x, part in plain.items()}
        pair = jnp.concatenate([plain[0], plain[1]], axis=1)
        field = stencil(value, 0, pair, d_ref.at[v], band_ref)
        store(f_ref, v, 0, field)
        total = products(field * two(w_ref, 0), pair)
        factor = []
        for x in range(2):
            near, far = (ref[owners, x, v].astype(jnp.float32) for ref in (near_ref, far_ref))
            parts = jnp.where(odd, near, far)
            factor.append(parts[0:1] + parts[1:2] + parts[2:3])
        joined = jnp.concatenate(
            [-value[0] * factor[0], (16.0 * value[0] - value[1]) * factor[1]], axis=1
        )
        total = total + products(joined, jnp.concatenate([plain[-2], plain[-1]], axis=1))
        cross_ref[...] += total


def upper_kernel(odd_ref, x_ref, near_ref, far_ref, d_ref, band_ref, f_ref):
    variables, rows = x_ref.shape[:2]
    owners = near_ref.shape[0] - 1
    odd = odd_ref[0] == 1
    for v in range(variables):
        plain = {x: x_ref[v, x] for x in range(rows - 4, rows)}
        for x in range(2):
            near = row_of(near_ref.at[:owners], x, v)
            plain[rows + x] = jnp.where(odd, far_ref[x, v], near)
        value = {x: part.astype(jnp.float32) for x, part in plain.items()}
        pair = jnp.concatenate([plain[rows - 2], plain[rows - 1]], axis=1)
        store(f_ref, v, 0, stencil(value, rows - 2, pair, d_ref.at[v], band_ref))


def band_matrix(width):
    shape = (2, width, 2, width)
    i, y, j, z = (lax.broadcasted_iota(jnp.int32, shape, axis) for axis in range(4))
    distance = jnp.abs(y - z)
    line = jnp.where(
        distance == 0, -60.0, jnp.where(distance == 1, 16.0, jnp.where(distance == 2, -1.0, 0.0))
    )
    return jnp.where(i == j, line, 0.0).reshape(2 * width, 2 * width).astype(jnp.bfloat16)


COST = {"inner": 1, "lower": 1, "upper": 1}


def stencil_call(kernel, name, block, span, pairs, cross, *operands, odd=None):
    _, _, size, width = block.shape
    field = jax.ShapeDtypeStruct((2, span, pairs, size, 2 * width), jnp.bfloat16)
    total = jax.ShapeDtypeStruct((size, size), jnp.float32)
    flags = [] if odd is None else [odd]
    return pl.pallas_call(
        kernel,
        in_specs=[pl.BlockSpec(memory_space=pltpu.SMEM)] * len(flags) + [VMEM] * (1 + len(operands)),
        out_specs=[VMEM, VMEM] if cross else VMEM,
        out_shape=[total, field] if cross else field,
        compiler_params=params(),
        cost_estimate=cost(COST[name]),
        name=name,
    )(*flags, block, *operands)


PANEL = 32
GROUP = 8


def lanes(value, width):
    return jnp.concatenate([value] * (width // value.shape[1]), axis=1)


def sublanes(value, height):
    return jnp.concatenate([value] * (height // value.shape[0]), axis=0)


def split3(value):
    high = value.astype(jnp.bfloat16)
    rest = value - high.astype(jnp.float32)
    middle = rest.astype(jnp.bfloat16)
    return high, middle, (rest - middle.astype(jnp.float32)).astype(jnp.bfloat16)


def eliminate(panel, start, at):
    height, size = panel.shape
    first = start + at
    sub = lax.broadcasted_iota(jnp.int32, (height, size), 0)
    lane = lax.broadcasted_iota(jnp.int32, (height, size), 1)
    sub1 = lax.broadcasted_iota(jnp.int32, (height, 128), 0)
    lane8 = lax.broadcasted_iota(jnp.int32, (8, size), 1)
    span = range(GROUP)
    columns = [jnp.broadcast_to(panel[:, first + i : first + i + 1], (height, 128)) for i in span]
    rows = [jnp.broadcast_to(panel[at + i : at + i + 1, :], (8, size)) for i in span]
    entry = {
        (i, k): jnp.broadcast_to(columns[k][at + i : at + i + 1, :], (8, 128))
        for i in span
        for k in range(i, GROUP)
    }
    inverse = []
    for i in span:
        inverse.append(1.0 / entry[i, i])
        rows[i] = jnp.where(lane8 == first + i, 1.0, rows[i])
        for k in range(i + 1, GROUP):
            factor = entry[i, k] * inverse[i]
            rows[k] = jnp.where(lane8 == first + i, 0.0, rows[k]) - lanes(factor, size) * rows[i]
            columns[k] = columns[k] - sublanes(factor, height) * columns[i]
            for j in range(i + 1, k + 1):
                entry[j, k] = entry[j, k] - factor * entry[i, j]
    rows = [
        jnp.where((lane8 > first + i) & (lane8 < first + GROUP), 0.0, rows[i]) for i in span
    ]
    done = at + GROUP
    result = jnp.where((lane >= first) & (lane < first + GROUP) & (sub >= done), 0.0, panel)
    for i in span:
        factor = jnp.where(sub1 >= done, columns[i] * sublanes(inverse[i], height), 0.0)
        result = result - lanes(factor, size) * sublanes(rows[i], height)
    for i in span:
        result = jnp.where(sub == at + i, sublanes(rows[i], height), result)
    return result, [entry[i, i] for i in span]


def rotation_panels(begin, stop, out_ref, work_ref):
    size = work_ref.shape[0]
    sub = lax.broadcasted_iota(jnp.int32, (PANEL, size), 0)
    lane = lax.broadcasted_iota(jnp.int32, (PANEL, size), 1)
    sub1 = lax.broadcasted_iota(jnp.int32, (PANEL, 128), 0)
    for start in range(begin, stop, PANEL):
        end = start + PANEL
        panel = work_ref[start:end, :]
        norm = jnp.zeros((PANEL, 128), jnp.float32)
        for at in range(0, PANEL, GROUP):
            panel, pivots = eliminate(panel, start, at)
            for i, pivot in enumerate(pivots):
                norm = jnp.where(sub1 == at + i, sublanes(lax.rsqrt(pivot), PANEL), norm)
        panel = panel * lanes(norm, size)
        panel = jnp.where((lane > start + sub) & (lane < end), 0.0, panel)
        out_ref[start:end, :] = jnp.where(lane < end, panel, 0.0)
        if end < size:
            high, middle, low = split3(panel)
            right = jnp.concatenate([high, middle, low, high, middle, high], axis=0)
            left = jnp.concatenate(
                [part[:, end:] for part in (high, high, high, middle, middle, low)], axis=0
            )
            update = lax.dot_general(
                left, right, (((0,), (0,)), ((), ())), preferred_element_type=jnp.float32
            )
            rest = work_ref[end:, :]
            place = lax.broadcasted_iota(jnp.int32, rest.shape, 1)
            work_ref[end:, :] = jnp.where((place >= start) & (place < end), 0.0, rest) - update


def rotation_first_kernel(scale, gram_ref, out_ref, work_ref):
    size = work_ref.shape[0]
    half = size // 2
    first, last = unpack(gram_ref[:half, :half] * scale, gram_ref[half : half + 1, :half] * scale)
    work_ref[:half, :half] = first
    work_ref[half:, half:] = last
    work_ref[:half, half:] = gram_ref[:half, half:] * scale
    work_ref[half:, :half] = jnp.zeros((half, half), jnp.float32)
    rotation_panels(0, half, out_ref, work_ref)


def rotation_last_kernel(before_ref, state_ref, out_ref, work_ref):
    size = work_ref.shape[0]
    half = size // 2
    out_ref[:half, :] = before_ref[...]
    work_ref[half:, :] = state_ref[half:, :]
    rotation_panels(half, size, out_ref, work_ref)


def rotation_first(packed, cell_count):
    size = packed.shape[1]
    return pl.pallas_call(
        lambda *refs: rotation_first_kernel(1.0 / cell_count, *refs),
        in_specs=[VMEM],
        out_specs=[VMEM, VMEM],
        out_shape=[
            jax.ShapeDtypeStruct((size // 2, size), jnp.float32),
            jax.ShapeDtypeStruct((size, size), jnp.float32),
        ],
        compiler_params=params(),
        cost_estimate=cost(1),
        name="rotation_first",
    )(packed)


def rotation_last(before, state):
    size = state.shape[0]
    return pl.pallas_call(
        rotation_last_kernel,
        in_specs=[VMEM, VMEM],
        out_specs=VMEM,
        out_shape=jax.ShapeDtypeStruct((size, size), jnp.float32),
        scratch_shapes=[pltpu.VMEM((size, size), jnp.float32)],
        compiler_params=params(),
        cost_estimate=cost(1),
        name="rotation_last",
    )(before, state)


def modes_kernel(first, r_ref, low_ref, mid_ref, top_ref, *refs):
    out_ref = refs[-1]
    high, low = split(r_ref[...])
    v = pl.program_id(0)
    width = mid_ref.shape[4] // 2
    places = [(low_ref, first + v, 0)]
    places += [(mid_ref, v, p) for p in range(mid_ref.shape[2])]
    places += [(top_ref, first + v, 0)]
    rows = []
    for ref, at, p in places:
        large, small = ref[0, at, p], ref[1, at, p]
        value = matmul(high, large) + matmul(high, small) + matmul(low, large)
        value = value.astype(out_ref.dtype)
        rows += [value[:, :width], value[:, width:]]
    out_ref[:, 0] = jnp.swapaxes(jnp.stack(rows, axis=0), 0, 1)


def modes_of(rotation, low, mid, top, first, before):
    variables, (_, span, pairs, size, width) = low.shape[1], mid.shape
    rows, width = 2 * pairs + 4, width // 2
    earlier = [] if before is None else [before]
    return pl.pallas_call(
        lambda *refs: modes_kernel(first, *refs),
        grid=(span,),
        in_specs=[pl.BlockSpec((size, size), lambda v: (0, 0))]
        + [VMEM] * 3
        + [pl.BlockSpec(memory_space=pl.ANY)] * len(earlier),
        out_specs=pl.BlockSpec((size, 1, rows, width), lambda v: (0, first + v, 0, 0)),
        out_shape=jax.ShapeDtypeStruct((size, variables, rows, width), jnp.bfloat16),
        input_output_aliases={4: 0} if earlier else {},
        compiler_params=params(),
        cost_estimate=cost(1 if before is None else 10 * size * size * rows * span * width),
        name="modes",
    )(rotation, low, mid, top, *earlier)


class Sum:
    def __init__(self, value, axis):
        self.axis, self.count = axis, lax.axis_size(axis)
        self.butterfly = self.count >= 2 and not self.count & (self.count - 1)
        if not self.butterfly:
            self.own = value
            return
        half = value.shape[0] // 2
        self.odd = lax.axis_index(axis) % 2 == 1
        first, second = value[:half], value[half:]
        self.own = jnp.where(self.odd, second, first) + self.swap(
            jnp.where(self.odd, first, second), 1
        )

    def swap(self, part, step):
        return lax.ppermute(part, self.axis, [(i, i ^ step) for i in range(self.count)])

    def steps(self):
        return [1 << k for k in range(1, self.count.bit_length() - 1)] if self.butterfly else []

    def add(self, step):
        self.own = self.own + self.swap(self.own, step)

    def result(self):
        if not self.butterfly:
            return lax.psum(self.own, self.axis)
        other = self.swap(self.own, 1)
        low, high = jnp.where(self.odd, other, self.own), jnp.where(self.odd, self.own, other)
        return jnp.concatenate([low, high], axis=0)


def shifted(value, axis, step):
    count = lax.axis_size(axis)
    pairs = [(i, i + step) for i in range(count) if 0 <= i + step < count]
    return lax.ppermute(value, axis, pairs)


def hop(value, axis, first, step):
    devices = lax.axis_size(axis)
    return lax.ppermute(
        value, axis, [(i, i + step) for i in range(first, devices, 2) if 0 <= i + step < devices]
    )


def lower_rows(block, weights, diffusivity, axis):
    devices = lax.axis_size(axis)
    _, rows, variables, count, width = block.shape
    odd = lax.axis_index(axis) % 2 == 1
    factor = weights[None, rows - 2 :] * (diffusivity[:, rows - 2 :] * (1.0 / 12.0))
    top = lax.reduce_precision(factor, 8, 7)
    middle = lax.reduce_precision(factor - top, 8, 7)
    parts = jnp.stack([top, middle, factor - top - middle], axis=2).astype(block.dtype)
    parts = parts.transpose(1, 0, 2, 3)
    parts = jnp.pad(parts, ((0, 0), (0, 0), (0, count - 3), (0, 0)))[None]
    near, far = [
        jnp.concatenate([lax.dynamic_slice_in_dim(block, start, 2, axis=1), parts], axis=0)
        for start in (jnp.where(odd, 0, rows - 2), rows - 2)
    ]
    near, far, block = lax.optimization_barrier((near, far, block))
    pairs = [(i, i + 1) for i in range(0, devices - 1, 2)]
    near = lax.ppermute(near, axis, pairs + [(b, a) for a, b in pairs])
    return block, near, hop(far, axis, 1, 1)


def on_device(snapshots, cell_weights, diffusivity):
    highest = lax.Precision.HIGHEST
    together = lax.optimization_barrier
    owners = lax.axis_size("gx")
    block = lax.all_to_all(relayout(snapshots, owners), "gx", 0, 0, tiled=True)
    if snapshots.shape[0] % 16:
        count, rows, variables, each, width = block.shape
        block = block.transpose(1, 2, 0, 3, 4).reshape(1, rows, variables, count * each, width)
    _, rows, variables, count, width = block.shape
    size, cell_count = block.shape[0] * count, rows * variables * width * owners
    band = band_matrix(width)
    half = variables - variables // 4
    spans = [span for span in (range(half), range(half, variables)) if len(span)]

    odd = (lax.axis_index("gx") % 2).astype(jnp.int32).reshape(1)
    block, near, far = lower_rows(block, cell_weights, diffusivity, "gx")
    block, near = together((block, near))
    packed, kept, first_rows = gram_of(block, cell_weights)
    cross = jnp.zeros((size, size), jnp.float32)
    mids = []

    def inner(span, kept, cross):
        cross, mid = stencil_call(
            functools.partial(inner_kernel, span), "inner", kept, len(span), rows // 2 - 2, True,
            cell_weights, diffusivity, band, cross,
        )
        mids.append(mid)
        return cross

    gram = Sum(packed, "gx")
    steps = gram.steps()
    kept, first_rows, gram.own = together((kept, first_rows, gram.own))
    above = hop(first_rows, "gx", 0, -1)
    for span in spans:
        if mids:
            kept, cross, gram.own = together((kept, cross, gram.own))
        cross = inner(span, kept, cross)
        if steps:
            gram.add(steps.pop(0))
    kept, cross, gram.own = together((kept, cross, gram.own))
    cross, bottom = stencil_call(
        lower_kernel, "lower", kept, variables, 1, True,
        near, far, cell_weights, diffusivity, band, cross, odd=odd,
    )
    cross = Sum(cross, "gx")
    while steps:
        gram.add(steps.pop(0))
    steps = cross.steps()
    if steps:
        cross.add(steps.pop(0))
    top = stencil_call(
        upper_kernel, "upper", kept, variables, 1, False, near, above, diffusivity, band, odd=odd
    )
    gram.own, top = together((gram.own, top))
    packed, cross.own = together((gram.result(), cross.own))
    state = rotation_first(packed, cell_count)
    if steps:
        cross.add(steps.pop(0))
    state, cross.own = together((state, cross.own))
    rotation = rotation_last(*state)
    while steps:
        cross.add(steps.pop(0))
    modes = None
    for span, mid in zip(spans, mids):
        if modes is not None:
            modes, cross.own = together((modes, cross.own))
        modes = modes_of(rotation, bottom, mid, top, span[0], modes)
    cross_total = cross.result() * (1.0 / cell_count)
    reduced = jnp.dot(
        jnp.dot(rotation, cross_total.T, precision=highest), rotation.T, precision=highest
    )
    return (modes, reduced)


def solution(mesh):
    in_specs = (
        P("gx", None, "groups", None),
        P(("groups", "gx"), None),
        P(None, ("groups", "gx"), None),
    )
    out_specs = (P(None, None, ("groups", "gx"), None), P("groups", None))
    return jax.shard_map(
        on_device, mesh=mesh, in_specs=in_specs, out_specs=out_specs, check_vma=False
    )
```

```python
import functools
import math

import jax
import jax.numpy as jnp
from jax import lax
from jax.experimental import pallas as pl
from jax.experimental.pallas import tpu as pltpu
from jax.sharding import PartitionSpec as P

VMEM_LIMIT = 24 * 1024 * 1024
NT = (((1,), (1,)), ((), ()))


def cost(flops):
    return pl.CostEstimate(flops=int(flops), bytes_accessed=1, transcendentals=0)


VMEM = pl.BlockSpec(memory_space=pltpu.VMEM)


def params():
    return pltpu.CompilerParams(vmem_limit_bytes=VMEM_LIMIT)


def split(value):
    high = value.astype(jnp.bfloat16)
    low = (value - high.astype(jnp.float32)).astype(jnp.bfloat16)
    return high, low


def matmul(a, b):
    return jnp.dot(a, b, preferred_element_type=jnp.float32)


def matmul_nt(a, b):
    return lax.dot_general(a, b, NT, preferred_element_type=jnp.float32)


def relayout_kernel(reads, writes, in_ref, out_ref, from_ref, to_ref, read_sems, write_sems):
    owners, rows, variables = to_ref.shape[:3]
    each_read, each_write = owners // reads, owners // writes
    arriving = []
    for i in range(reads):
        span = pl.ds(i * each_read * rows, each_read * rows)
        arriving.append(
            pltpu.make_async_copy(in_ref.at[:, :, span], from_ref.at[:, :, span], read_sems.at[i])
        )
        arriving[i].start()
    leaving = []
    for i in range(writes):
        for owner in range(i * each_write, (i + 1) * each_write):
            if owner % each_read == 0:
                arriving[owner // each_read].wait()
            for v in range(variables):
                block = from_ref[:, v, owner * rows : (owner + 1) * rows]
                to_ref[owner, :, v] = jnp.swapaxes(block, 0, 1)
        span = pl.ds(i * each_write, each_write)
        leaving.append(pltpu.make_async_copy(to_ref.at[span], out_ref.at[span], write_sems.at[i]))
        leaving[i].start()
    for copy in leaving:
        copy.wait()


def relayout(snapshots, owners):
    count, variables, cells, width = snapshots.shape
    rows = cells // owners
    if count % 16 or rows % 16:
        block = snapshots.reshape(count, variables, owners, rows, width)
        return block.transpose(2, 3, 1, 0, 4)
    reads, writes = math.gcd(owners, 4), math.gcd(owners, 8)
    shape = (owners, rows, variables, count, width)
    return pl.pallas_call(
        functools.partial(relayout_kernel, reads, writes),
        in_specs=[pl.BlockSpec(memory_space=pl.ANY)],
        out_specs=pl.BlockSpec(memory_space=pl.ANY),
        out_shape=jax.ShapeDtypeStruct(shape, snapshots.dtype),
        scratch_shapes=[
            pltpu.VMEM(snapshots.shape, snapshots.dtype),
            pltpu.VMEM(shape, snapshots.dtype),
            pltpu.SemaphoreType.DMA((reads,)),
            pltpu.SemaphoreType.DMA((writes,)),
        ],
        compiler_params=pltpu.CompilerParams(vmem_limit_bytes=60 * 1024 * 1024),
        name="relayout",
    )(snapshots)


def row_of(ref, x, v):
    value = ref[:, x, v]
    return value.reshape(value.shape[0] * value.shape[1], value.shape[2])


def pack(gram):
    half = gram.shape[0] // 2
    sub = lax.broadcasted_iota(jnp.int32, (half, half), 0)
    lane = lax.broadcasted_iota(jnp.int32, (half, half), 1)
    first, last = gram[:half, :half], gram[half:, half:]
    diagonal = jnp.sum(jnp.where(lane == sub, first, 0.0), axis=0, keepdims=True)
    mixed = jnp.where(lane > sub, first, last)
    top = jnp.concatenate([mixed, gram[:half, half:]], axis=1)
    return top, jnp.broadcast_to(jnp.concatenate([diagonal, diagonal], axis=1), (16, 2 * half))


def unpack(mixed, diagonal):
    half = mixed.shape[0]
    sub = lax.broadcasted_iota(jnp.int32, (half, half), 0)
    lane = lax.broadcasted_iota(jnp.int32, (half, half), 1)
    upper = jnp.where(lane > sub, mixed, 0.0)
    lower = jnp.where(lane < sub, mixed, 0.0)
    first = jnp.where(lane == sub, diagonal, upper + upper.T)
    last = jnp.where(lane == sub, mixed, lower + lower.T)
    return first, last


def gram_kernel(x_ref, w_ref, out_ref, keep_ref, first_ref, total_ref):
    rows, each = x_ref.shape[1:3]
    size = total_ref.shape[0]

    @pl.when(pl.program_id(0) == 0)
    def _():
        total_ref[...] = jnp.zeros_like(total_ref)

    total = None
    for v in range(each):
        for first in range(0, rows, 4):
            group = range(first, first + 4)
            plain = [row_of(x_ref, x, v) for x in group]
            at = pl.program_id(0) * each + v
            for x in group:
                keep_ref[at, x] = plain[x - first]
                if x < 2:
                    first_ref[x, at] = plain[x - first]
            plain = jnp.concatenate(plain, axis=1)
            weight = jnp.concatenate([w_ref[x : x + 1, :] for x in group], axis=1)
            high, low = split(plain.astype(jnp.float32) * weight)
            term = matmul_nt(high, plain) + matmul_nt(low, plain)
            total = term if total is None else total + term
    total_ref[...] += total

    @pl.when(pl.program_id(0) == pl.num_programs(0) - 1)
    def _():
        top, diagonal = pack(total_ref[...])
        out_ref[: size // 2, :] = top
        out_ref[size // 2 :, :] = diagonal


def gram_of(block, weights):
    owners, rows, variables, count, width = block.shape
    size = owners * count
    each = 2 if variables % 2 == 0 else 1
    return pl.pallas_call(
        gram_kernel,
        grid=(variables // each,),
        in_specs=[
            pl.BlockSpec((owners, rows, each, count, width), lambda v: (0, 0, v, 0, 0)),
            pl.BlockSpec((rows, width), lambda v: (0, 0)),
        ],
        out_specs=[pl.BlockSpec((size // 2 + 16, size), lambda v: (0, 0)), VMEM, VMEM],
        out_shape=[
            jax.ShapeDtypeStruct((size // 2 + 16, size), jnp.float32),
            jax.ShapeDtypeStruct((variables, rows, size, width), block.dtype),
            jax.ShapeDtypeStruct((2, variables, size, width), block.dtype),
        ],
        scratch_shapes=[pltpu.VMEM((size, size), jnp.float32)],
        compiler_params=params(),
        cost_estimate=cost(2e9),
        name="gram",
    )(block, weights)


def along_x(lower, upper, centre):
    near = [part for part in (lower[1], upper[0]) if part is not None]
    far = [part for part in (lower[0], upper[1]) if part is not None]
    value = 16.0 * sum(near[1:], near[0]) if near else jnp.zeros_like(centre)
    return value - sum(far[1:], far[0]) if far else value


def two(ref, x):
    return jnp.concatenate([ref[x : x + 1, :], ref[x + 1 : x + 2, :]], axis=1)


def stencil(value, x, pair, d_ref, band_ref):
    sides = [
        along_x((value.get(k - 2), value.get(k - 1)), (value.get(k + 1), value.get(k + 2)), value[k])
        for k in (x, x + 1)
    ]
    both = matmul(pair, band_ref[...]) + jnp.concatenate(sides, axis=1)
    return both * (two(d_ref, x) * (1.0 / 12.0))


def products(left, right):
    term = matmul_nt(jnp.concatenate(split(left), axis=0), right)
    half = term.shape[0] // 2
    return term[:half] + term[half:]


def store(f_ref, v, p, field):
    f_ref[0, v, p], f_ref[1, v, p] = split(field)


def inner_kernel(span, x_ref, w_ref, d_ref, band_ref, before_ref, cross_ref, f_ref):
    rows = x_ref.shape[1]
    cross_ref[...] = before_ref[...]
    for place, v in enumerate(span):
        plain = [x_ref[v, x] for x in range(rows)]
        value = {x: part.astype(jnp.float32) for x, part in enumerate(plain)}
        total = None
        for x in range(2, rows, 2):
            pair = jnp.concatenate(plain[x : x + 2], axis=1)
            field = stencil(value, x, pair, d_ref.at[v], band_ref)
            if x < rows - 2:
                store(f_ref, place, x // 2 - 1, field)
            term = products(field * two(w_ref, x), pair)
            total = term if total is None else total + term
        cross_ref[...] += total


def lower_kernel(odd_ref, x_ref, near_ref, far_ref, w_ref, d_ref, band_ref, before_ref, cross_ref, f_ref):
    variables, owners = x_ref.shape[0], near_ref.shape[0] - 1
    odd = odd_ref[0] == 1
    cross_ref[...] = before_ref[...]
    for v in range(variables):
        plain = {x: x_ref[v, x] for x in range(4)}
        for x in range(2):
            near, far = (row_of(ref.at[:owners], x, v) for ref in (near_ref, far_ref))
            plain[x - 2] = jnp.where(odd, near, far)
        value = {x: part.astype(jnp.float32) for x, part in plain.items()}
        pair = jnp.concatenate([plain[0], plain[1]], axis=1)
        field = stencil(value, 0, pair, d_ref.at[v], band_ref)
        store(f_ref, v, 0, field)
        total = products(field * two(w_ref, 0), pair)
        factor = []
        for x in range(2):
            near, far = (ref[owners, x, v].astype(jnp.float32) for ref in (near_ref, far_ref))
            parts = jnp.where(odd, near, far)
            factor.append(parts[0:1] + parts[1:2] + parts[2:3])
        joined = jnp.concatenate(
            [-value[0] * factor[0], (16.0 * value[0] - value[1]) * factor[1]], axis=1
        )
        total = total + products(joined, jnp.concatenate([plain[-2], plain[-1]], axis=1))
        cross_ref[...] += total


def upper_kernel(odd_ref, x_ref, near_ref, far_ref, d_ref, band_ref, f_ref):
    variables, rows = x_ref.shape[:2]
    owners = near_ref.shape[0] - 1
    odd = odd_ref[0] == 1
    for v in range(variables):
        plain = {x: x_ref[v, x] for x in range(rows - 4, rows)}
        for x in range(2):
            near = row_of(near_ref.at[:owners], x, v)
            plain[rows + x] = jnp.where(odd, far_ref[x, v], near)
        value = {x: part.astype(jnp.float32) for x, part in plain.items()}
        pair = jnp.concatenate([plain[rows - 2], plain[rows - 1]], axis=1)
        store(f_ref, v, 0, stencil(value, rows - 2, pair, d_ref.at[v], band_ref))


def band_matrix(width):
    shape = (2, width, 2, width)
    i, y, j, z = (lax.broadcasted_iota(jnp.int32, shape, axis) for axis in range(4))
    distance = jnp.abs(y - z)
    line = jnp.where(
        distance == 0, -60.0, jnp.where(distance == 1, 16.0, jnp.where(distance == 2, -1.0, 0.0))
    )
    return jnp.where(i == j, line, 0.0).reshape(2 * width, 2 * width).astype(jnp.bfloat16)


COST = {"inner": 1, "lower": 1, "upper": 1}


def stencil_call(kernel, name, block, span, pairs, cross, *operands, odd=None):
    _, _, size, width = block.shape
    field = jax.ShapeDtypeStruct((2, span, pairs, size, 2 * width), jnp.bfloat16)
    total = jax.ShapeDtypeStruct((size, size), jnp.float32)
    flags = [] if odd is None else [odd]
    return pl.pallas_call(
        kernel,
        in_specs=[pl.BlockSpec(memory_space=pltpu.SMEM)] * len(flags) + [VMEM] * (1 + len(operands)),
        out_specs=[VMEM, VMEM] if cross else VMEM,
        out_shape=[total, field] if cross else field,
        compiler_params=params(),
        cost_estimate=cost(COST[name]),
        name=name,
    )(*flags, block, *operands)


PANEL = 32
GROUP = 8


def lanes(value, width):
    return jnp.concatenate([value] * (width // value.shape[1]), axis=1)


def sublanes(value, height):
    return jnp.concatenate([value] * (height // value.shape[0]), axis=0)


def split3(value):
    high = value.astype(jnp.bfloat16)
    rest = value - high.astype(jnp.float32)
    middle = rest.astype(jnp.bfloat16)
    return high, middle, (rest - middle.astype(jnp.float32)).astype(jnp.bfloat16)


def eliminate(panel, start, at):
    height, size = panel.shape
    first = start + at
    sub = lax.broadcasted_iota(jnp.int32, (height, size), 0)
    lane = lax.broadcasted_iota(jnp.int32, (height, size), 1)
    sub1 = lax.broadcasted_iota(jnp.int32, (height, 128), 0)
    lane8 = lax.broadcasted_iota(jnp.int32, (8, size), 1)
    span = range(GROUP)
    columns = [jnp.broadcast_to(panel[:, first + i : first + i + 1], (height, 128)) for i in span]
    rows = [jnp.broadcast_to(panel[at + i : at + i + 1, :], (8, size)) for i in span]
    entry = {
        (i, k): jnp.broadcast_to(columns[k][at + i : at + i + 1, :], (8, 128))
        for i in span
        for k in range(i, GROUP)
    }
    inverse = []
    for i in span:
        inverse.append(1.0 / entry[i, i])
        rows[i] = jnp.where(lane8 == first + i, 1.0, rows[i])
        for k in range(i + 1, GROUP):
            factor = entry[i, k] * inverse[i]
            rows[k] = jnp.where(lane8 == first + i, 0.0, rows[k]) - lanes(factor, size) * rows[i]
            columns[k] = columns[k] - sublanes(factor, height) * columns[i]
            for j in range(i + 1, k + 1):
                entry[j, k] = entry[j, k] - factor * entry[i, j]
    rows = [
        jnp.where((lane8 > first + i) & (lane8 < first + GROUP), 0.0, rows[i]) for i in span
    ]
    done = at + GROUP
    result = jnp.where((lane >= first) & (lane < first + GROUP) & (sub >= done), 0.0, panel)
    for i in span:
        factor = jnp.where(sub1 >= done, columns[i] * sublanes(inverse[i], height), 0.0)
        result = result - lanes(factor, size) * sublanes(rows[i], height)
    for i in span:
        result = jnp.where(sub == at + i, sublanes(rows[i], height), result)
    return result, [entry[i, i] for i in span]


def rotation_panels(begin, stop, out_ref, work_ref):
    size = work_ref.shape[0]
    sub = lax.broadcasted_iota(jnp.int32, (PANEL, size), 0)
    lane = lax.broadcasted_iota(jnp.int32, (PANEL, size), 1)
    sub1 = lax.broadcasted_iota(jnp.int32, (PANEL, 128), 0)
    for start in range(begin, stop, PANEL):
        end = start + PANEL
        panel = work_ref[start:end, :]
        norm = jnp.zeros((PANEL, 128), jnp.float32)
        for at in range(0, PANEL, GROUP):
            panel, pivots = eliminate(panel, start, at)
            for i, pivot in enumerate(pivots):
                norm = jnp.where(sub1 == at + i, sublanes(lax.rsqrt(pivot), PANEL), norm)
        panel = panel * lanes(norm, size)
        panel = jnp.where((lane > start + sub) & (lane < end), 0.0, panel)
        out_ref[start:end, :] = jnp.where(lane < end, panel, 0.0)
        if end < size:
            high, middle, low = split3(panel)
            right = jnp.concatenate([high, middle, low, high, middle, high], axis=0)
            left = jnp.concatenate(
                [part[:, end:] for part in (high, high, high, middle, middle, low)], axis=0
            )
            update = lax.dot_general(
                left, right, (((0,), (0,)), ((), ())), preferred_element_type=jnp.float32
            )
            rest = work_ref[end:, :]
            place = lax.broadcasted_iota(jnp.int32, rest.shape, 1)
            work_ref[end:, :] = jnp.where((place >= start) & (place < end), 0.0, rest) - update


def rotation_kernel(scale, gram_ref, out_ref, work_ref):
    size = work_ref.shape[0]
    half = size // 2
    first, last = unpack(gram_ref[:half, :half] * scale, gram_ref[half : half + 1, :half] * scale)
    work_ref[:half, :half] = first
    work_ref[half:, half:] = last
    work_ref[:half, half:] = gram_ref[:half, half:] * scale
    work_ref[half:, :half] = jnp.zeros((half, half), jnp.float32)
    rotation_panels(0, size, out_ref, work_ref)


def rotation_of(packed, cell_count):
    size = packed.shape[1]
    return pl.pallas_call(
        lambda *refs: rotation_kernel(1.0 / cell_count, *refs),
        in_specs=[VMEM],
        out_specs=VMEM,
        out_shape=jax.ShapeDtypeStruct((size, size), jnp.float32),
        scratch_shapes=[pltpu.VMEM((size, size), jnp.float32)],
        compiler_params=params(),
        cost_estimate=cost(1),
        name="rotation",
    )(packed)


def modes_kernel(first, r_ref, low_ref, mid_ref, top_ref, *refs):
    out_ref = refs[-1]
    high, low = split(r_ref[...])
    v = pl.program_id(0)
    width = mid_ref.shape[4] // 2
    places = [(low_ref, first + v, 0)]
    places += [(mid_ref, v, p) for p in range(mid_ref.shape[2])]
    places += [(top_ref, first + v, 0)]
    rows = []
    for ref, at, p in places:
        large, small = ref[0, at, p], ref[1, at, p]
        value = matmul(high, large) + matmul(high, small) + matmul(low, large)
        value = value.astype(out_ref.dtype)
        rows += [value[:, :width], value[:, width:]]
    out_ref[:, 0] = jnp.swapaxes(jnp.stack(rows, axis=0), 0, 1)


def modes_of(rotation, low, mid, top, first, before):
    variables, (_, span, pairs, size, width) = low.shape[1], mid.shape
    rows, width = 2 * pairs + 4, width // 2
    earlier = [] if before is None else [before]
    return pl.pallas_call(
        lambda *refs: modes_kernel(first, *refs),
        grid=(span,),
        in_specs=[pl.BlockSpec((size, size), lambda v: (0, 0))]
        + [VMEM] * 3
        + [pl.BlockSpec(memory_space=pl.ANY)] * len(earlier),
        out_specs=pl.BlockSpec((size, 1, rows, width), lambda v: (0, first + v, 0, 0)),
        out_shape=jax.ShapeDtypeStruct((size, variables, rows, width), jnp.bfloat16),
        input_output_aliases={4: 0} if earlier else {},
        compiler_params=params(),
        cost_estimate=cost(1 if before is None else 10 * size * size * rows * span * width),
        name="modes",
    )(rotation, low, mid, top, *earlier)


class Sum:
    def __init__(self, value, axis):
        self.axis, self.count = axis, lax.axis_size(axis)
        self.butterfly = self.count >= 2 and not self.count & (self.count - 1)
        if not self.butterfly:
            self.own = value
            return
        half = value.shape[0] // 2
        self.odd = lax.axis_index(axis) % 2 == 1
        first, second = value[:half], value[half:]
        self.own = jnp.where(self.odd, second, first) + self.swap(
            jnp.where(self.odd, first, second), 1
        )

    def swap(self, part, step):
        return lax.ppermute(part, self.axis, [(i, i ^ step) for i in range(self.count)])

    def steps(self):
        return [1 << k for k in range(1, self.count.bit_length() - 1)] if self.butterfly else []

    def add(self, step):
        self.own = self.own + self.swap(self.own, step)

    def result(self):
        if not self.butterfly:
            return lax.psum(self.own, self.axis)
        other = self.swap(self.own, 1)
        low, high = jnp.where(self.odd, other, self.own), jnp.where(self.odd, self.own, other)
        return jnp.concatenate([low, high], axis=0)


def shifted(value, axis, step):
    count = lax.axis_size(axis)
    pairs = [(i, i + step) for i in range(count) if 0 <= i + step < count]
    return lax.ppermute(value, axis, pairs)


def hop(value, axis, first, step):
    devices = lax.axis_size(axis)
    return lax.ppermute(
        value, axis, [(i, i + step) for i in range(first, devices, 2) if 0 <= i + step < devices]
    )


def lower_rows(block, weights, diffusivity, axis):
    devices = lax.axis_size(axis)
    _, rows, variables, count, width = block.shape
    odd = lax.axis_index(axis) % 2 == 1
    factor = weights[None, rows - 2 :] * (diffusivity[:, rows - 2 :] * (1.0 / 12.0))
    top = lax.reduce_precision(factor, 8, 7)
    middle = lax.reduce_precision(factor - top, 8, 7)
    parts = jnp.stack([top, middle, factor - top - middle], axis=2).astype(block.dtype)
    parts = parts.transpose(1, 0, 2, 3)
    parts = jnp.pad(parts, ((0, 0), (0, 0), (0, count - 3), (0, 0)))[None]
    near, far = [
        jnp.concatenate([lax.dynamic_slice_in_dim(block, start, 2, axis=1), parts], axis=0)
        for start in (jnp.where(odd, 0, rows - 2), rows - 2)
    ]
    near, far, block = lax.optimization_barrier((near, far, block))
    pairs = [(i, i + 1) for i in range(0, devices - 1, 2)]
    near = lax.ppermute(near, axis, pairs + [(b, a) for a, b in pairs])
    return block, near, hop(far, axis, 1, 1)


def on_device(snapshots, cell_weights, diffusivity):
    highest = lax.Precision.HIGHEST
    together = lax.optimization_barrier
    owners = lax.axis_size("gx")
    block = lax.all_to_all(relayout(snapshots, owners), "gx", 0, 0, tiled=True)
    if snapshots.shape[0] % 16:
        count, rows, variables, each, width = block.shape
        block = block.transpose(1, 2, 0, 3, 4).reshape(1, rows, variables, count * each, width)
    _, rows, variables, count, width = block.shape
    size, cell_count = block.shape[0] * count, rows * variables * width * owners
    band = band_matrix(width)
    half = variables - variables // 4
    spans = [span for span in (range(half), range(half, variables)) if len(span)]

    odd = (lax.axis_index("gx") % 2).astype(jnp.int32).reshape(1)
    block, near, far = lower_rows(block, cell_weights, diffusivity, "gx")
    block, near = together((block, near))
    packed, kept, first_rows = gram_of(block, cell_weights)
    cross = jnp.zeros((size, size), jnp.float32)
    mids = []

    def inner(span, kept, cross):
        cross, mid = stencil_call(
            functools.partial(inner_kernel, span), "inner", kept, len(span), rows // 2 - 2, True,
            cell_weights, diffusivity, band, cross,
        )
        mids.append(mid)
        return cross

    gram = Sum(packed, "gx")
    steps = gram.steps()
    kept, first_rows, gram.own = together((kept, first_rows, gram.own))
    above = hop(first_rows, "gx", 0, -1)
    for span in spans:
        if mids:
            kept, cross, gram.own = together((kept, cross, gram.own))
        cross = inner(span, kept, cross)
        if steps:
            gram.add(steps.pop(0))
    kept, cross, gram.own = together((kept, cross, gram.own))
    cross, bottom = stencil_call(
        lower_kernel, "lower", kept, variables, 1, True,
        near, far, cell_weights, diffusivity, band, cross, odd=odd,
    )
    cross = Sum(cross, "gx")
    while steps:
        gram.add(steps.pop(0))
    steps = cross.steps()
    if steps:
        cross.add(steps.pop(0))
    top = stencil_call(
        upper_kernel, "upper", kept, variables, 1, False, near, above, diffusivity, band, odd=odd
    )
    gram.own, top = together((gram.own, top))
    packed, cross.own = together((gram.result(), cross.own))
    rotation = rotation_of(packed, cell_count)
    if steps:
        cross.add(steps.pop())
    rotation, cross.own = together((rotation, cross.own))
    while steps:
        cross.add(steps.pop(0))
    modes = None
    for span, mid in zip(spans, mids):
        if modes is not None:
            modes, cross.own = together((modes, cross.own))
        modes = modes_of(rotation, bottom, mid, top, span[0], modes)
    cross_total = cross.result() * (1.0 / cell_count)
    reduced = jnp.dot(
        jnp.dot(rotation, cross_total.T, precision=highest), rotation.T, precision=highest
    )
    return (modes, reduced)


def solution(mesh):
    in_specs = (
        P("gx", None, "groups", None),
        P(("groups", "gx"), None),
        P(None, ("groups", "gx"), None),
    )
    out_specs = (P(None, None, ("groups", "gx"), None), P("groups", None))
    return jax.shard_map(
        on_device, mesh=mesh, in_specs=in_specs, out_specs=out_specs, check_vma=False
    )
```
